1024 devices in a mesh: lat: 32 (over x, y), lon: 32 (over z, core).
Axes of the slice: x: 4, y: 8, z: 16, core: 2. Of those that a mesh axis runs over, the one named last changes fastest.
Arguments:
- right_side: float32 [128, 4096, 512], P('lat', 'lon'), may hold values from -80 to 80
- eofs: bfloat16 [128, 512, 64], P('lat'), may hold values from -0.5 to 0.5
- spectral_gain: float32 [64, 512], P('lon'), may hold values from 0.2 to 2
- diffusivity: float32 [64], replicated, may hold values from 0.05 to 0.25
- flags: int32 [128, 4096], P('lat', 'lon'), may hold values from 0 to 3
- counts: int32 [128, 4096], P('lat', 'lon'), may hold values from 0 to 8
Outputs:
- solution_field: float32 [128, 4096, 512], P('lat', 'lon')
- residual: float32 [128, 4096, 512], P('lat', 'lon')
The draws below stay inside these ranges and needn't reach their ends.
All inputs are finite; a program needn't handle non-finite values.
Results may differ from the reference program's by a relative error of at most 0.035.
Values may be sent and summed in bfloat16 or wider, within the bound.
A program may use at most 64 MiB of HBM per device.

```python
import math
import jax
import jax.numpy as jnp
from jax import lax

COLV = 512
MODES = 64
KEEP = 512
ITERS = 2
NLAT = 128
NLON = 4096


def draw_right_side(key, part):
    key = jax.random.fold_in(key, 7)
    key_base, key_rough = jax.random.split(key)
    lat_frac = jnp.arange(NLAT, dtype=jnp.float32) / NLAT
    lon_frac = jnp.arange(NLON, dtype=jnp.float32) / NLON
    trend = jnp.exp(math.log(10.0) * (0.5 * lat_frac[:, None] + 0.5 * lon_frac[None, :]))
    rough = jnp.exp(jax.random.uniform(key_rough, (NLAT, NLON), jnp.float32, -0.69, 0.69))
    base = jnp.clip(jax.random.normal(key_base, (NLAT, NLON, COLV), jnp.float32), -3.9, 3.9)
    return (base * (trend * rough)[:, :, None]).astype(jnp.float32)


def set_ends(array, stream_key, least, high):
    index_at = [jax.random.randint(jax.random.fold_in(stream_key, axis), (), 0, length) for axis, length in enumerate(array.shape)]
    longest = array.shape.index(max(array.shape))
    beside = index_at[:longest] + [(index_at[longest] + 1) % array.shape[longest]] + index_at[longest + 1:]
    return array.at[tuple(index_at)].set(least).at[tuple(beside)].set(high)


def block_scale(own_key, extent, pieces, least, top_value):
    def one(axis_at, shards_of):
        steps = jax.random.uniform(jax.random.fold_in(jax.random.fold_in(own_key, 6), axis_at), (shards_of,), jnp.float32, least / len(pieces), top_value / len(pieces))
        return jnp.repeat(jnp.exp(steps), extent[axis_at] // shards_of).reshape((-1,) + (1,) * (len(extent) - axis_at - 1))

    gain = one(*pieces[0])
    for cut in pieces[1:]:
        gain = gain * one(*cut)
    return gain


def gaussian(key, dims, spread, reach, cuts=(), kind=jnp.bfloat16):
    result = jax.random.normal(key, dims, jnp.float32) * spread
    if len(cuts) > 0:
        result = block_scale(key, dims, cuts, -0.22, 0.18) * result
    return jnp.clip(result, min=-reach, max=reach).astype(kind)


def setup_inputs(seed: int = 0) -> dict:
    seeds = jax.random.split(jax.random.key(seed), 7)
    return {
        "right_side": draw_right_side(jax.random.fold_in(seeds[6], 71), 0),
        "eofs": gaussian(seeds[1], (NLAT, COLV, MODES), (2 * MODES) ** -0.5, 0.5, ((0, 32),)),
        "spectral_gain": jnp.clip(jnp.exp(math.log(2.0) - 2.3025851 * jax.random.uniform(seeds[2], (MODES, KEEP), jnp.float32) ** block_scale(seeds[2], (MODES, KEEP), ((0, 32),), -0.2, 0.2)), 0.2, 2.0),
        "diffusivity": jnp.clip(jnp.exp(jax.random.uniform(seeds[3], (MODES,), jnp.float32, math.log(0.05), math.log(0.25))), 0.05, 0.25),
        "flags": set_ends(jax.random.randint(seeds[4], (NLAT, NLON), 0, 4), jax.random.fold_in(seeds[4], 1), 0, 3).astype(jnp.int32),
        "counts": set_ends(jax.random.randint(seeds[5], (NLAT, NLON), 0, 9), jax.random.fold_in(seeds[5], 1), 0, 8).astype(jnp.int32),
    }


def weight_of(flags, counts):
    factor = (flags == 0).astype(jnp.float32) + 0.5 * (flags == 1).astype(jnp.float32) + 0.25 * (flags == 2).astype(jnp.float32)
    return factor * counts.astype(jnp.float32) * 0.25


def spectral_table(first, rows, nlon, keep):
    points = first + jnp.arange(rows, dtype=jnp.int32)
    waves = jnp.arange(keep, dtype=jnp.int32)
    phase = (points[:, None] * waves[None, :]) % nlon
    angle = (2.0 * math.pi / nlon) * phase.astype(jnp.float32)
    return jnp.concatenate([jnp.cos(angle), jnp.sin(angle)], axis=1).astype(jnp.bfloat16)


def gain_table(spectral_gain, nlon):
    keep = spectral_gain.shape[1]
    waves = jnp.arange(keep, dtype=jnp.int32)
    factor = jnp.where(waves == 0, 1.0, 2.0).astype(jnp.float32) / nlon
    scaled = spectral_gain * factor[None, :]
    return jnp.concatenate([scaled, scaled], axis=1)


def diffuse(field, kappa):
    padded = jnp.pad(field, ((1, 1), (0, 0), (0, 0)))
    return padded[1:-1] + kappa * (padded[2:] - 2.0 * padded[1:-1] + padded[:-2])


def operate(field, eofs, gain_all, kappa, obs_weight, table):
    weighted = (obs_weight * field).astype(jnp.bfloat16)
    modes = lax.map(lambda pair: jnp.dot(pair[0], pair[1], preferred_element_type=jnp.float32), (weighted, eofs))
    modes = jnp.transpose(modes, (0, 2, 1))
    modes = diffuse(modes, kappa)
    diffused = diffuse(modes, kappa).astype(jnp.bfloat16)
    coef = jnp.dot(diffused.reshape(NLAT * MODES, NLON), table, preferred_element_type=jnp.float32)
    scaled = (coef.reshape(NLAT, MODES, 2 * KEEP) * gain_all[None]).astype(jnp.bfloat16)
    smoothed = jnp.dot(scaled.reshape(NLAT * MODES, 2 * KEEP), table.T, preferred_element_type=jnp.float32)
    smoothed = smoothed.reshape(NLAT, MODES, NLON).astype(jnp.bfloat16)
    expanded = lax.map(lambda pair: jnp.dot(pair[0].T, pair[1].T, preferred_element_type=jnp.float32), (smoothed, eofs))
    return field + obs_weight * expanded


def reference(right_side, eofs, spectral_gain, diffusivity, flags, counts):
    obs_weight = weight_of(flags, counts)[:, :, None]
    table = spectral_table(0, NLON, NLON, KEEP)
    gain_all = gain_table(spectral_gain, NLON)
    kappa = diffusivity[None, :, None]
    solution_field = jnp.zeros_like(right_side)
    residual = right_side
    direction = right_side
    norm_now = jnp.sum(residual * residual)
    for step in range(ITERS):
        image = operate(direction, eofs, gain_all, kappa, obs_weight, table)
        alpha = norm_now / jnp.sum(direction * image)
        solution_field = solution_field + alpha * direction
        residual = residual - alpha * image
        if step + 1 < ITERS:
            norm_next = jnp.sum(residual * residual)
            direction = residual + (norm_next / norm_now) * direction
            norm_now = norm_next
    return solution_field, residual
```

```python
import math

import jax
import jax.numpy as jnp
import numpy as np
from jax import lax
from jax.experimental import pallas as pl
from jax.experimental.pallas import tpu as pltpu
from jax.sharding import PartitionSpec as P

MESH = pl.DeviceIdType.MESH
F32, BF16 = jnp.float32, jnp.bfloat16
ROWS, MODES, COLV, NLON, KEEP = 4, 64, 512, 4096, 512
LON, ZS, PTS = 32, 16, 128
K1 = 9
SPEC = K1 * MODES
GROUP = 16
OWNER_STEP = LON // ROWS

C1, C3, RT = math.cos(math.pi / 8), math.sin(math.pi / 8), math.sqrt(0.5)


def tables():
    kk = np.arange(32)
    signed = np.concatenate([kk, -1 - kk])
    j = np.arange(256)
    angle = 2.0 * np.pi * ((j[:, None] * signed[None, :]) % 256) / 256.0
    cos, sin = np.cos(angle), np.sin(angle)
    re_in = np.concatenate([cos[:, :32], sin[:, :32], cos[:, 32:], sin[:, 32:]], axis=1)
    im_in = np.concatenate([-sin[:, :32], cos[:, :32], -sin[:, 32:], cos[:, 32:]], axis=1)
    wave = np.stack([re_in.reshape(2, PTS, 128), im_in.reshape(2, PTS, 128)], axis=1)
    wave = wave.reshape(2, 2 * PTS, 128)
    k1 = np.arange(K1)
    phase = 2.0 * np.pi * ((k1[:, None] * j[None, :]) % NLON) / NLON
    twist = np.stack([np.cos(phase), np.sin(phase)], axis=1)
    twist = twist.reshape(2 * K1, 2, PTS).transpose(1, 0, 2)
    pick = np.zeros((KEEP, K1, 128))
    for one in range(K1):
        for lane in range(128):
            part, at = lane // 32, lane % 32
            if part < 2:
                k = one + 16 * at
            elif 1 <= one <= 7:
                k = 16 * at + 16 - one
            else:
                continue
            pick[k, one, lane] = (1.0 if k == 0 else 2.0) / NLON
    pick = pick.reshape(KEEP, K1 * 128)
    return (
        jnp.asarray(wave.astype(jnp.bfloat16)),
        jnp.asarray(twist.astype(np.float32)),
        jnp.asarray(pick.astype(jnp.bfloat16)),
    )


def cosines(p):
    e = [p[0] + p[8], p[1] + p[7], p[2] + p[6], p[3] + p[5], p[4]]
    o = [p[0] - p[8], p[1] - p[7], p[2] - p[6], p[3] - p[5]]
    f0, f1 = e[0] + e[4], e[1] + e[3]
    f02 = f0 + e[2]
    g0, g1 = e[0] - e[4], RT * (e[1] - e[3])
    o2 = RT * o[2]
    a, b = o[0] + o2, o[0] - o2
    u, v = C1 * o[1] + C3 * o[3], C3 * o[1] - C1 * o[3]
    return [f02 + f1, a + u, g0 + g1, b + v, f0 - e[2], b - v, g0 - g1, a - u, f02 - f1]


def sines(q):
    h = [None, q[1] + q[7], q[2] + q[6], q[3] + q[5], q[4]]
    d = [None, q[1] - q[7], q[2] - q[6], q[3] - q[5]]
    r = RT * (d[1] + d[3])
    h2 = RT * h[2]
    m, n = h2 + h[4], h2 - h[4]
    u, v = C3 * h[1] + C1 * h[3], C1 * h[1] - C3 * h[3]
    return [None, u + m, r + d[2], v + n, d[1] - d[3], v - n, r - d[2], u - m]


def column_of(row, size):
    at = lax.broadcasted_iota(jnp.int32, (size, size), 0)
    to = lax.broadcasted_iota(jnp.int32, (size, size), 1)
    spread = jnp.where(at == to, jnp.broadcast_to(row, (size, size)), 0.0)
    return jnp.sum(spread, axis=1, keepdims=True)


def by_lane(values):
    part = values[:, 0:128] + values[:, 128:256] + values[:, 256:384] + values[:, 384:512]
    return jnp.sum(part, axis=0, keepdims=True)


def kernel(
    lats,
    b_hbm, e_hbm, gain_ref, kappa_ref, flags_ref, counts_ref, wave_hbm, twist_hbm, pick_hbm,
    x_hbm, r_hbm,
    b, e, wave, twist, pick, y0, halo_out, halo_in, halo_in2,
    aux_g, aux_w, got_g, got_w, to_owner, rows_in, zbuf, bbuf, gains, y1,
    s_out, f_out, s_in, f_in, tbuf, ubuf, part, ar1, mid, ar2, xo, ro,
    ld, aux_s, aux_r, halo_s, halo_r, own_s, own_r, ret_s, ret_r, ar_s, ar_r, out_s,
):
    lat, me = lax.axis_index("lat"), lax.axis_index("lon")
    owner = lax.rem(me, OWNER_STEP) == 0
    my_row = lax.div(me, OWNER_STEP)

    barrier = pltpu.get_barrier_semaphore()

    def greet_lon(o, carry):
        pl.semaphore_signal(
            barrier, inc=1, device_id=(lat, lax.rem(me + o, LON)), device_id_type=MESH
        )
        return carry

    def greet_lat(o, carry):
        pl.semaphore_signal(
            barrier, inc=1, device_id=(lax.rem(lat + o, lats), me), device_id_type=MESH
        )
        return carry

    loads = [
        pltpu.make_async_copy(b_hbm, b, ld.at[0]),
        pltpu.make_async_copy(e_hbm, e, ld.at[1]),
    ]
    for load in loads:
        load.start()
    lax.fori_loop(1, LON, greet_lon, 0)
    lax.fori_loop(1, lats, greet_lat, 0)

    owner_loads = [
        pltpu.make_async_copy(wave_hbm, wave, ld.at[2]),
        pltpu.make_async_copy(twist_hbm, twist, ld.at[3]),
        pltpu.make_async_copy(pick_hbm, pick, ld.at[4]),
    ]

    @pl.when(owner)
    def _():
        for load in owner_loads:
            load.start()

    flags = flags_ref[...]
    factor = (
        (flags == 0).astype(F32) + 0.5 * (flags == 1).astype(F32) + 0.25 * (flags == 2).astype(F32)
    )
    weight = factor * counts_ref[...].astype(F32) * 0.25
    w_col = [column_of(weight[r : r + 1, :], PTS) for r in range(ROWS)]
    kappa = column_of(kappa_ref[...], MODES)
    for mode in range(2):
        for quarter in range(4):
            at = mode * 4 + quarter
            aux_g[at : at + 1, :] = gain_ref[mode : mode + 1, quarter * 128 : quarter * 128 + 128]
    for r in range(ROWS):
        aux_w[r] = jnp.broadcast_to(weight[r : r + 1, :], (8, PTS))

    for load in loads:
        load.wait()
    for r in range(ROWS):
        weighted = (w_col[r] * b[r]).astype(BF16)
        modes = jnp.dot(weighted, e[r], preferred_element_type=F32).T
        y0[r] = modes
        halo_out[r] = modes.astype(BF16)

    pl.semaphore_wait(barrier, LON - 1 + lats - 1)

    down, up = lax.rem(lat + lats - 1, lats), lax.rem(lat + 1, lats)

    def halo(source, target, at):
        copies = [
            pltpu.make_async_remote_copy(
                source.at[pl.ds(2 * way, 2)], target.at[1 - way],
                halo_s.at[at + way], halo_r.at[at + way],
                device_id=(peer, me), device_id_type=MESH,
            )
            for way, peer in ((0, down), (1, up))
        ]
        for copy in copies:
            copy.start()
        return copies

    def diffuse(rows, halos):
        low, high = lat > 0, lat < lats - 1
        ext = [jnp.where(low, halos[0, i].astype(F32), 0.0) for i in range(2)]
        ext += rows
        ext += [jnp.where(high, halos[1, i].astype(F32), 0.0) for i in range(2)]
        once = [
            ext[i] + kappa * (ext[i + 1] - 2.0 * ext[i] + ext[i - 1]) for i in range(1, 7)
        ]
        once[0] = jnp.where(low, once[0], 0.0)
        once[5] = jnp.where(high, once[5], 0.0)
        return [
            once[i] + kappa * (once[i + 1] - 2.0 * once[i] + once[i - 1]) for i in range(1, 5)
        ]

    first_halo = halo(halo_out, halo_in, 0)

    for r in range(ROWS):
        at = r * OWNER_STEP

        @pl.when(me != at)
        def _():
            for source, target, which in ((aux_g, got_g, 0), (aux_w.at[r], got_w, 1)):
                pltpu.make_async_remote_copy(
                    source, target.at[pl.ds(pl.multiple_of(8 * me, 8), 8)],
                    aux_s.at[which], aux_r.at[which],
                    device_id=(lat, at), device_id_type=MESH,
                ).start()

        @pl.when(me == at)
        def _():
            got_g[pl.ds(pl.multiple_of(8 * me, 8), 8), :] = aux_g[...]
            got_w[pl.ds(pl.multiple_of(8 * me, 8), 8), :] = aux_w[r]

    for copy in first_halo:
        copy.wait()
    diffused = diffuse([y0[r] for r in range(ROWS)], halo_in)
    for r in range(ROWS):
        to_owner[r] = diffused[r].astype(BF16)
    for r in range(ROWS):
        at = r * OWNER_STEP

        @pl.when(me != at)
        def _():
            pltpu.make_async_remote_copy(
                to_owner.at[r], rows_in.at[me], own_s.at[0], own_r.at[0],
                device_id=(lat, at), device_id_type=MESH,
            ).start()

        @pl.when(me == at)
        def _():
            rows_in[me] = to_owner[r]

    def settle(buffer, count, semaphore):
        view = buffer.at[pl.ds(0, count)]
        pltpu.make_async_copy(view, view, semaphore).wait()

    def smooth(source, target):
        def forward(g, carry):
            c, rows = lax.div(g, 4), pl.ds(pl.multiple_of(lax.rem(g, 4) * GROUP, GROUP), GROUP)
            x = [source[2 * z + c, rows, :].astype(F32) for z in range(ZS)]
            p = [x[0]] + [x[z] + x[16 - z] for z in range(1, 8)] + [x[8]]
            q = [None] + [x[z] - x[16 - z] for z in range(1, 8)]
            real, imag = cosines(p), sines(q)
            for k1 in range(K1):
                to = pl.ds(pl.multiple_of(k1 * MODES + lax.rem(g, 4) * GROUP, GROUP), GROUP)
                if k1 == 0:
                    re, im = real[0], jnp.zeros_like(real[0])
                else:
                    cos = twist[c, pl.ds(2 * k1, 1), :]
                    sin = twist[c, pl.ds(2 * k1 + 1, 1), :]
                    if k1 == 8:
                        re, im = real[8] * cos, real[8] * sin
                    else:
                        re = real[k1] * cos - imag[k1] * sin
                        im = real[k1] * sin + imag[k1] * cos
                zbuf[c, to, 0:PTS] = re.astype(BF16)
                zbuf[c, to, PTS : 2 * PTS] = im.astype(BF16)
            return carry

        lax.fori_loop(0, 8, forward, 0)
        for chunk in range(3):
            rows = pl.ds(chunk * 192, 192)
            coef = jnp.dot(zbuf[0, rows, :], wave[0], preferred_element_type=F32)
            coef = coef + jnp.dot(zbuf[1, rows, :], wave[1], preferred_element_type=F32)
            scaled = (coef * gains[rows, :]).astype(BF16)
            for c in range(2):
                bbuf[c, rows, :] = lax.dot_general(
                    scaled, wave[c], (((1,), (1,)), ((), ())), preferred_element_type=F32
                )

        def inverse(g, carry):
            c, rows = lax.div(g, 4), pl.ds(pl.multiple_of(lax.rem(g, 4) * GROUP, GROUP), GROUP)
            real, imag = [], [None]
            for k1 in range(K1):
                at = pl.ds(pl.multiple_of(k1 * MODES + lax.rem(g, 4) * GROUP, GROUP), GROUP)
                re = bbuf[c, at, 0:PTS]
                if k1 == 0:
                    real.append(re)
                    continue
                im = bbuf[c, at, PTS : 2 * PTS]
                cos = twist[c, pl.ds(2 * k1, 1), :]
                sin = twist[c, pl.ds(2 * k1 + 1, 1), :]
                real.append(re * cos + im * sin)
                if k1 < 8:
                    imag.append(im * cos - re * sin)
            even, odd = cosines(real), sines(imag)
            target[c, rows, :] = even[0].astype(BF16)
            target[16 + c, rows, :] = even[8].astype(BF16)
            for z in range(1, 8):
                target[2 * z + c, rows, :] = (even[z] + odd[z]).astype(BF16)
                target[2 * (16 - z) + c, rows, :] = (even[z] - odd[z]).astype(BF16)
            return carry

        lax.fori_loop(0, 8, inverse, 0)

    def give_back(source, target, which):
        def send(o):
            peer = lax.rem(me + o, LON)
            pltpu.make_async_remote_copy(
                source.at[peer], target.at[my_row], ret_s.at[which], ret_r.at[which],
                device_id=(lat, peer), device_id_type=MESH,
            ).start()

        def pair(o, carry):
            send(16 - o)
            send(16 + o)
            return carry

        send(16)
        lax.fori_loop(1, 16, pair, 0)
        target[my_row] = source[me]

    @pl.when(owner)
    def _():
        for load in owner_loads:
            load.wait()
        transposed = e[my_row].astype(F32).T.astype(BF16)
        gram = jnp.dot(transposed, e[my_row], preferred_element_type=F32)
        gram_high = gram.astype(BF16)
        gram_low = (gram - gram_high.astype(F32)).astype(BF16)
        gram_both = jnp.concatenate([gram_high.astype(F32), gram_low.astype(F32)], axis=1).astype(BF16)

        settle(got_g.reshape(LON, 8, 128), LON - 1, aux_r.at[0])
        settle(got_w.reshape(LON, 8, 128), LON - 1, aux_r.at[1])
        spread = jnp.concatenate([got_g[pl.ds(q, MODES, stride=4), :] for q in range(4)], axis=1)
        first = spread.astype(BF16)
        rest = spread - first.astype(F32)
        second = rest.astype(BF16)
        third = (rest - second.astype(F32)).astype(BF16)
        for k1 in range(K1):
            lanes = pl.ds(k1 * 128, 128)
            total = jnp.dot(first, pick[:, lanes], preferred_element_type=F32)
            total = total + jnp.dot(second, pick[:, lanes], preferred_element_type=F32)
            total = total + jnp.dot(third, pick[:, lanes], preferred_element_type=F32)
            gains[pl.ds(k1 * MODES, MODES), :] = total

        settle(rows_in, LON - 1, own_r.at[0])
        smooth(rows_in, s_out)
        give_back(s_out, s_in, 0)

        for z in range(ZS):
            pair = jnp.concatenate([s_out[2 * z], s_out[2 * z + 1]], axis=1)
            product = jnp.dot(
                gram_both, jnp.concatenate([pair, pair], axis=0), preferred_element_type=F32
            )
            for c in range(2):
                row = got_w[pl.ds(8 * (2 * z + c), 1), :]
                y1[2 * z + c] = product[:, c * PTS : c * PTS + PTS] * (row * row)
        smooth(y1, f_out)
        give_back(f_out, f_in, 1)

    def expand(values, r):
        return w_col[r] * lax.dot_general(
            values.T.astype(BF16), e[r], (((1,), (1,)), ((), ())), preferred_element_type=F32
        )

    def arrived(buffer, which):
        @pl.when(owner)
        def _():
            settle(buffer, ROWS - 1, ret_r.at[which])

        @pl.when(jnp.logical_not(owner))
        def _():
            settle(buffer, ROWS, ret_r.at[which])

    arrived(s_in, 0)
    sums = [jnp.zeros((1, PTS), F32) for _ in range(4)]
    for r in range(ROWS):
        t = expand(s_in[r].astype(F32), r)
        tbuf[r] = t
        values = b[r]
        sums[0] = sums[0] + by_lane(values * values)
        sums[1] = sums[1] + by_lane(values * t)
        sums[2] = sums[2] + by_lane(t * t)

    arrived(f_in, 1)
    second_halo = halo(f_in, halo_in2, 2)
    for copy in second_halo:
        copy.wait()
    diffused = diffuse([f_in[r].astype(F32) for r in range(ROWS)], halo_in2)
    for r in range(ROWS):
        u = expand(diffused[r], r)
        ubuf[r] = u
        sums[3] = sums[3] + by_lane(tbuf[r] * u)
    part[...] = jnp.concatenate(sums + [jnp.zeros((4, PTS), F32)], axis=0)

    def share(source, target, mine, count, which, device):
        def send(o, carry):
            pltpu.make_async_remote_copy(
                source, target.at[mine], ar_s.at[which], ar_r.at[which],
                device_id=device(o), device_id_type=MESH,
            ).start()
            return carry

        lax.fori_loop(1, count, send, 0)
        target[mine] = source[...]
        settle(target, count - 1, ar_r.at[which])
        total = target[0]
        for i in range(1, count):
            total = total + target[i]
        return total

    mid[...] = share(part, ar1, me, LON, 0, lambda o: (lat, lax.rem(me + o, LON)))
    total = share(mid, ar2, lat, lats, 1, lambda o: (lax.rem(lat + o, lats), me))
    total = jnp.sum(total, axis=1, keepdims=True)
    norm = total[0:1]
    m1, m2, m3 = total[1:2] / norm, total[2:3] / norm, total[3:4] / norm
    alpha = 1.0 / (1.0 + m1)
    spread2 = m2 - m1 * m1
    spread3 = m3 - 3.0 * m1 * m2 + 2.0 * m1 * m1 * m1
    beta = alpha * alpha * spread2
    alpha_next = alpha * spread2 / (spread2 * (1.0 - beta) + alpha * spread3)
    along = alpha * m1 + beta
    x_b, x_t = alpha + alpha_next * along, -alpha_next * alpha
    r_b = alpha * m1 - alpha_next * along
    r_t = -(alpha + alpha_next * (along - alpha))
    r_u = alpha_next * alpha

    writes = []
    for r in range(ROWS):
        xo[r] = x_b * b[r] + x_t * tbuf[r]
        ro[r] = r_b * b[r] + r_t * tbuf[r] + r_u * ubuf[r]
        for source, target, at in ((xo, x_hbm, 0), (ro, r_hbm, 1)):
            write = pltpu.make_async_copy(source.at[r], target.at[r], out_s.at[at, r])
            write.start()
            writes.append(write)
    for write in writes:
        write.wait()

    @pl.when(owner)
    def _():
        settle(aux_w, ROWS - 1, aux_s.at[0])
        settle(aux_w, ROWS - 1, aux_s.at[1])
        settle(to_owner, ROWS - 1, own_s.at[0])
        settle(s_out, LON - 1, ret_s.at[0])
        settle(f_out, LON - 1, ret_s.at[1])

    @pl.when(jnp.logical_not(owner))
    def _():
        settle(aux_w, ROWS, aux_s.at[0])
        settle(aux_w, ROWS, aux_s.at[1])
        settle(to_owner, ROWS, own_s.at[0])

    settle(ar1, LON - 1, ar_s.at[0])
    settle(ar2, lats - 1, ar_s.at[1])


def local(right_side, eofs, spectral_gain, diffusivity, flags, counts):
    lats = lax.axis_size("lat")
    wave, twist, pick = tables()
    anywhere = pl.BlockSpec(memory_space=pl.ANY)
    vmem = pl.BlockSpec(memory_space=pltpu.VMEM)
    like = jax.ShapeDtypeStruct(right_side.shape, F32)
    dma, vm = pltpu.SemaphoreType.DMA, pltpu.VMEM

    def whole(*args):
        kernel(lats, *args)

    return pl.pallas_call(
        whole,
        out_shape=(like, like),
        in_specs=[anywhere, anywhere, vmem, vmem, vmem, vmem, anywhere, anywhere, anywhere],
        out_specs=(anywhere, anywhere),
        scratch_shapes=[
            vm((ROWS, PTS, COLV), F32),
            vm((ROWS, COLV, MODES), BF16),
            vm((2, 2 * PTS, 128), BF16),
            vm((2, 2 * K1, PTS), F32),
            vm((KEEP, K1 * 128), BF16),
            vm((ROWS, MODES, PTS), F32),
            vm((ROWS, MODES, PTS), BF16),
            vm((2, 2, MODES, PTS), BF16),
            vm((2, 2, MODES, PTS), BF16),
            vm((8, 128), F32),
            vm((ROWS, 8, PTS), F32),
            vm((LON * 8, 128), F32),
            vm((LON * 8, PTS), F32),
            vm((ROWS, MODES, PTS), BF16),
            vm((LON, MODES, PTS), BF16),
            vm((2, SPEC, 2 * PTS), BF16),
            vm((2, SPEC, 2 * PTS), F32),
            vm((SPEC, 128), F32),
            vm((LON, MODES, PTS), F32),
            vm((LON, MODES, PTS), BF16),
            vm((LON, MODES, PTS), BF16),
            vm((ROWS, MODES, PTS), BF16),
            vm((ROWS, MODES, PTS), BF16),
            vm((ROWS, PTS, COLV), F32),
            vm((ROWS, PTS, COLV), F32),
            vm((8, PTS), F32),
            vm((LON, 8, PTS), F32),
            vm((8, PTS), F32),
            vm((lats, 8, PTS), F32),
            vm((ROWS, PTS, COLV), F32),
            vm((ROWS, PTS, COLV), F32),
            dma((5,)),
            dma((2,)),
            dma((2,)),
            dma((4,)),
            dma((4,)),
            dma((1,)),
            dma((1,)),
            dma((2,)),
            dma((2,)),
            dma((2,)),
            dma((2,)),
            dma((2, ROWS)),
        ],
        compiler_params=pltpu.CompilerParams(
            collective_id=0, has_side_effects=True, vmem_limit_bytes=40 * 2**20
        ),
    )(
        right_side, eofs, spectral_gain, diffusivity.reshape(1, MODES), flags, counts,
        wave, twist, pick,
    )


def solution(mesh):
    in_specs = (
        P("lat", "lon", None),
        P("lat", None, None),
        P("lon", None),
        P(),
        P("lat", "lon"),
        P("lat", "lon"),
    )
    out_specs = (P("lat", "lon", None), P("lat", "lon", None))
    return jax.shard_map(local, mesh=mesh, in_specs=in_specs, out_specs=out_specs, check_vma=False)
```

```python
import math

import jax
import jax.numpy as jnp
import numpy as np
from jax import lax
from jax.experimental import pallas as pl
from jax.experimental.pallas import tpu as pltpu
from jax.sharding import PartitionSpec as P

MESH = pl.DeviceIdType.MESH
F32, BF16 = jnp.float32, jnp.bfloat16
ROWS, MODES, COLV, NLON, KEEP = 4, 64, 512, 4096, 512
LON, ZS, PTS = 32, 16, 128
K1 = 9
SPEC = K1 * MODES
GROUP = 16
OWNER_STEP = LON // ROWS

C1, C3, RT = math.cos(math.pi / 8), math.sin(math.pi / 8), math.sqrt(0.5)


def tables():
    kk = np.arange(32)
    signed = np.concatenate([kk, -1 - kk])
    j = np.arange(256)
    angle = 2.0 * np.pi * ((j[:, None] * signed[None, :]) % 256) / 256.0
    cos, sin = np.cos(angle), np.sin(angle)
    re_in = np.concatenate([cos[:, :32], sin[:, :32], cos[:, 32:], sin[:, 32:]], axis=1)
    im_in = np.concatenate([-sin[:, :32], cos[:, :32], -sin[:, 32:], cos[:, 32:]], axis=1)
    wave = np.stack([re_in.reshape(2, PTS, 128), im_in.reshape(2, PTS, 128)], axis=1)
    wave = wave.reshape(2, 2 * PTS, 128)
    k1 = np.arange(K1)
    phase = 2.0 * np.pi * ((k1[:, None] * j[None, :]) % NLON) / NLON
    twist = np.stack([np.cos(phase), np.sin(phase)], axis=1)
    twist = twist.reshape(2 * K1, 2, PTS).transpose(1, 0, 2)
    pick = np.zeros((KEEP, K1, 128))
    for one in range(K1):
        for lane in range(128):
            part, at = lane // 32, lane % 32
            if part < 2:
                k = one + 16 * at
            elif 1 <= one <= 7:
                k = 16 * at + 16 - one
            else:
                continue
            pick[k, one, lane] = (1.0 if k == 0 else 2.0) / NLON
    pick = pick.transpose(1, 0, 2)
    return (
        jnp.asarray(wave.astype(jnp.bfloat16)),
        jnp.asarray(twist.astype(np.float32)),
        jnp.asarray(pick.astype(jnp.bfloat16)),
    )


def cosines(p):
    e = [p[0] + p[8], p[1] + p[7], p[2] + p[6], p[3] + p[5], p[4]]
    o = [p[0] - p[8], p[1] - p[7], p[2] - p[6], p[3] - p[5]]
    f0, f1 = e[0] + e[4], e[1] + e[3]
    f02 = f0 + e[2]
    g0, g1 = e[0] - e[4], RT * (e[1] - e[3])
    o2 = RT * o[2]
    a, b = o[0] + o2, o[0] - o2
    u, v = C1 * o[1] + C3 * o[3], C3 * o[1] - C1 * o[3]
    return [f02 + f1, a + u, g0 + g1, b + v, f0 - e[2], b - v, g0 - g1, a - u, f02 - f1]


def sines(q):
    h = [None, q[1] + q[7], q[2] + q[6], q[3] + q[5], q[4]]
    d = [None, q[1] - q[7], q[2] - q[6], q[3] - q[5]]
    r = RT * (d[1] + d[3])
    h2 = RT * h[2]
    m, n = h2 + h[4], h2 - h[4]
    u, v = C3 * h[1] + C1 * h[3], C1 * h[1] - C3 * h[3]
    return [None, u + m, r + d[2], v + n, d[1] - d[3], v - n, r - d[2], u - m]


def column_of(row, size):
    at = lax.broadcasted_iota(jnp.int32, (size, size), 0)
    to = lax.broadcasted_iota(jnp.int32, (size, size), 1)
    spread = jnp.where(at == to, jnp.broadcast_to(row, (size, size)), 0.0)
    return jnp.sum(spread, axis=1, keepdims=True)


def by_lane(values):
    part = values[:, 0:128] + values[:, 128:256] + values[:, 256:384] + values[:, 384:512]
    return jnp.sum(part, axis=0, keepdims=True)


def kernel(
    lats,
    b_hbm, e_hbm, gain_hbm, kappa_hbm, flags_hbm, counts_hbm, wave_hbm, twist_hbm, pick_hbm,
    b, tbuf, ubuf, coefs,
    e, gain_ref, kappa_ref, flags_ref, counts_ref, wave, twist, pick,
    y0, halo_out, halo_in, halo_in2,
    aux_g, aux_w, got_g, got_w, to_owner, raw_in, rows_in, zbuf, bbuf, gains, y1,
    spec, spec_out, spec_in, s_out, f_out, s_in, f_in, part, ar1, mid, ar2,
    ld, aux_s, aux_r, halo_s, halo_r, own_s, own_r, spec_s, spec_r, ret_s, ret_r, ar_s, ar_r,
):
    lat, me = lax.axis_index("lat"), lax.axis_index("lon")
    owner = lax.rem(me, OWNER_STEP) == 0
    other = jnp.logical_not(owner)
    place, odd = lax.div(me, OWNER_STEP), lax.rem(lat, 2)

    def row_at(spot):
        return spot + odd * (ROWS - 1 - 2 * spot)

    my_row = row_at(place)
    down, up = lax.rem(lat + lats - 1, lats), lax.rem(lat + 1, lats)

    small = [
        pltpu.make_async_copy(source, target, ld.at[at])
        for at, (source, target) in enumerate(
            [
                (flags_hbm, flags_ref),
                (counts_hbm, counts_ref),
                (kappa_hbm, kappa_ref),
                (gain_hbm, gain_ref),
            ]
        )
    ]
    loads = [pltpu.make_async_copy(e_hbm, e, ld.at[4])]
    loads += [pltpu.make_async_copy(b_hbm.at[r], b.at[r], ld.at[5 + r]) for r in range(ROWS)]
    for load in small + loads:
        load.start()
    owner_loads = [
        pltpu.make_async_copy(wave_hbm, wave, ld.at[9]),
        pltpu.make_async_copy(twist_hbm, twist, ld.at[10]),
        pltpu.make_async_copy(pick_hbm, pick, ld.at[11]),
    ]

    barrier = pltpu.get_barrier_semaphore()

    def greet(device):
        pl.semaphore_signal(barrier, inc=1, device_id=device, device_id_type=MESH)

    @pl.when(owner)
    def _():
        def greet_lon(o, carry):
            greet((lat, lax.rem(me + o, LON)))
            return carry

        def greet_lat(o, carry):
            greet((lax.rem(lat + o, lats), me))
            return carry

        lax.fori_loop(1, LON, greet_lon, 0)
        lax.fori_loop(1, lats, greet_lat, 0)
        for load in owner_loads:
            load.start()

    @pl.when(other)
    def _():
        for spot in range(ROWS):
            greet((lat, spot * OWNER_STEP))
        greet((down, me))
        greet((up, me))

    for load in small:
        load.wait()
    flags = flags_ref[...]
    factor = (
        (flags == 0).astype(F32) + 0.5 * (flags == 1).astype(F32) + 0.25 * (flags == 2).astype(F32)
    )
    weight = factor * counts_ref[...].astype(F32) * 0.25
    w_col = [column_of(weight[r : r + 1, :], PTS) for r in range(ROWS)]
    kappa = column_of(kappa_ref[...], MODES)
    for mode in range(2):
        for quarter in range(4):
            at = mode * 4 + quarter
            aux_g[at : at + 1, :] = gain_ref[mode : mode + 1, quarter * 128 : quarter * 128 + 128]

    loads[0].wait()
    norm_part = jnp.zeros((1, PTS), F32)
    for r in range(ROWS):
        loads[1 + r].wait()
        weighted = (w_col[r] * b[r]).astype(BF16)
        modes = lax.dot_general(
            e[r], weighted, (((1,), (1,)), ((), ())), preferred_element_type=F32
        )
        y0[r] = modes
        halo_out[r] = modes.astype(BF16)
        norm_part = norm_part + by_lane(b[r] * b[r])
    for r in range(ROWS):
        aux_w[r] = jnp.concatenate([weight[r : r + 1, :], norm_part], axis=0)

    @pl.when(owner)
    def _():
        pl.semaphore_wait(barrier, LON - 1 + lats - 1)

    @pl.when(other)
    def _():
        pl.semaphore_wait(barrier, ROWS + 2)

    def halo(source, target, at):
        copies = [
            pltpu.make_async_remote_copy(
                source.at[pl.ds(2 * way, 2)], target.at[1 - way],
                halo_s.at[at + way], halo_r.at[at + way],
                device_id=(peer, me), device_id_type=MESH,
            )
            for way, peer in ((0, down), (1, up))
        ]
        for copy in copies:
            copy.start()
        return copies

    def diffuse(rows, halos):
        low, high = lat > 0, lat < lats - 1
        ext = [jnp.where(low, halos[0, i].astype(F32), 0.0) for i in range(2)]
        ext += rows
        ext += [jnp.where(high, halos[1, i].astype(F32), 0.0) for i in range(2)]
        once = [
            ext[i] + kappa * (ext[i + 1] - 2.0 * ext[i] + ext[i - 1]) for i in range(1, 7)
        ]
        once[0] = jnp.where(low, once[0], 0.0)
        once[5] = jnp.where(high, once[5], 0.0)
        return [
            once[i] + kappa * (once[i + 1] - 2.0 * once[i] + once[i - 1]) for i in range(1, 5)
        ]

    first_halo = halo(halo_out, halo_in, 0)

    def to_owners(sends):
        for spot in range(ROWS):
            at, row = spot * OWNER_STEP, row_at(spot)

            @pl.when(me != at)
            def _():
                for source, target, sent, got in sends(row):
                    pltpu.make_async_remote_copy(
                        source, target, sent, got, device_id=(lat, at), device_id_type=MESH
                    ).start()

            @pl.when(me == at)
            def _():
                for source, target, sent, got in sends(row):
                    target[...] = source[...]

    mine8 = pl.ds(pl.multiple_of(8 * me, 8), 8)
    to_owners(
        lambda row: (
            (halo_out.at[row], raw_in.at[me], own_s.at[0], own_r.at[0]),
            (aux_g, got_g.at[mine8], aux_s.at[0], aux_r.at[0]),
            (aux_w.at[row], got_w.at[me], aux_s.at[1], aux_r.at[1]),
        )
    )
    for copy in first_halo:
        copy.wait()
    diffused = diffuse([y0[r] for r in range(ROWS)], halo_in)
    for r in range(ROWS):
        to_owner[r] = diffused[r].astype(BF16)
    to_owners(lambda row: ((to_owner.at[row], rows_in.at[me], own_s.at[1], own_r.at[1]),))

    def settle(buffer, count, semaphore):
        view = buffer.at[pl.ds(0, count)]
        pltpu.make_async_copy(view, view, semaphore).wait()

    def forward(source):
        def one(g, carry):
            c, rows = lax.div(g, 4), pl.ds(pl.multiple_of(lax.rem(g, 4) * GROUP, GROUP), GROUP)
            x = [source[2 * z + c, rows, :].astype(F32) for z in range(ZS)]
            p = [x[0]] + [x[z] + x[16 - z] for z in range(1, 8)] + [x[8]]
            q = [None] + [x[z] - x[16 - z] for z in range(1, 8)]
            real, imag = cosines(p), sines(q)
            for k1 in range(K1):
                to = pl.ds(pl.multiple_of(k1 * MODES + lax.rem(g, 4) * GROUP, GROUP), GROUP)
                if k1 == 0:
                    re, im = real[0], jnp.zeros_like(real[0])
                else:
                    cos = twist[c, pl.ds(2 * k1, 1), :]
                    sin = twist[c, pl.ds(2 * k1 + 1, 1), :]
                    if k1 == 8:
                        re, im = real[8] * cos, real[8] * sin
                    else:
                        re = real[k1] * cos - imag[k1] * sin
                        im = real[k1] * sin + imag[k1] * cos
                zbuf[c, to, 0:PTS] = re.astype(BF16)
                zbuf[c, to, PTS : 2 * PTS] = im.astype(BF16)
            return carry

        lax.fori_loop(0, 8, one, 0)

    def coefficients(rows):
        coef = jnp.dot(zbuf[0, rows, :], wave[0], preferred_element_type=F32)
        return coef + jnp.dot(zbuf[1, rows, :], wave[1], preferred_element_type=F32)

    def back(coef, rows):
        scaled = (coef * gains[rows, :]).astype(BF16)
        for c in range(2):
            bbuf[c, rows, :] = lax.dot_general(
                scaled, wave[c], (((1,), (1,)), ((), ())), preferred_element_type=F32
            )

    chunks = [pl.ds(at * 192, 192) for at in range(3)]

    def inverse(target):
        def one(g, carry):
            c, rows = lax.div(g, 4), pl.ds(pl.multiple_of(lax.rem(g, 4) * GROUP, GROUP), GROUP)
            real, imag = [], [None]
            for k1 in range(K1):
                at = pl.ds(pl.multiple_of(k1 * MODES + lax.rem(g, 4) * GROUP, GROUP), GROUP)
                re = bbuf[c, at, 0:PTS]
                if k1 == 0:
                    real.append(re)
                    continue
                im = bbuf[c, at, PTS : 2 * PTS]
                cos = twist[c, pl.ds(2 * k1, 1), :]
                sin = twist[c, pl.ds(2 * k1 + 1, 1), :]
                real.append(re * cos + im * sin)
                if k1 < 8:
                    imag.append(im * cos - re * sin)
            even, odds = cosines(real), sines(imag)
            target[c, rows, :] = even[0].astype(BF16)
            target[16 + c, rows, :] = even[8].astype(BF16)
            for z in range(1, 8):
                target[2 * z + c, rows, :] = (even[z] + odds[z]).astype(BF16)
                target[2 * (16 - z) + c, rows, :] = (even[z] - odds[z]).astype(BF16)
            return carry

        lax.fori_loop(0, 8, one, 0)

    def give(source_at, target, semaphores):
        def send(o):
            peer = lax.rem(me + o, LON)
            pltpu.make_async_remote_copy(
                source_at(peer), target, semaphores[0], semaphores[1],
                device_id=(lat, peer), device_id_type=MESH,
            ).start()

        def pair(o, carry):
            send(16 - o)
            send(16 + o)
            return carry

        send(16)
        lax.fori_loop(1, 16, pair, 0)

    @pl.when(owner)
    def _():
        for load in owner_loads:
            load.wait()
        mine = e[my_row]
        gram = lax.dot_general(mine, mine, (((1,), (1,)), ((), ())), preferred_element_type=F32)
        gram_high = gram.astype(BF16)
        gram_low = (gram - gram_high.astype(F32)).astype(BF16)
        gram_both = jnp.concatenate(
            [gram_high.astype(F32), gram_low.astype(F32)], axis=1
        ).astype(BF16)

        settle(got_g.reshape(LON, 8, 128), LON - 1, aux_r.at[0])
        settle(got_w, LON - 1, aux_r.at[1])
        spread = jnp.concatenate([got_g[pl.ds(q, MODES, stride=4), :] for q in range(4)], axis=1)
        first = spread.astype(BF16)
        rest = spread - first.astype(F32)
        second = rest.astype(BF16)
        third = (rest - second.astype(F32)).astype(BF16)
        for k1 in range(K1):
            total = jnp.dot(first, pick[k1], preferred_element_type=F32)
            total = total + jnp.dot(second, pick[k1], preferred_element_type=F32)
            total = total + jnp.dot(third, pick[k1], preferred_element_type=F32)
            gains[pl.ds(k1 * MODES, MODES), :] = total
        norm_sum = got_w[0, 1:2, :]
        for source in range(1, LON):
            norm_sum = norm_sum + got_w[source, 1:2, :]

        settle(rows_in, LON - 1, own_r.at[1])
        forward(rows_in)
        for rows in chunks:
            back(coefficients(rows), rows)
        inverse(s_out)

        for z in range(ZS):
            pair = jnp.concatenate([s_out[2 * z], s_out[2 * z + 1]], axis=1)
            product = jnp.dot(
                gram_both, jnp.concatenate([pair, pair], axis=0), preferred_element_type=F32
            )
            for c in range(2):
                row = got_w[2 * z + c, 0:1, :]
                y1[2 * z + c] = product[:, c * PTS : c * PTS + PTS] * (row * row)
        forward(y1)
        for rows in chunks:
            coef = coefficients(rows)
            spec[rows, :] = coef
            spec_out[rows, :] = coef.astype(BF16)

        lowest, highest = lax.div(ROWS - 1 - my_row, ROWS - 1), lax.div(my_row, ROWS - 1)
        turn = 1 - 2 * odd
        before = (
            lax.rem(lat - lowest + lats, lats), OWNER_STEP * (place - turn * (1 - lowest))
        )
        after = (
            lax.rem(lat + highest, lats), OWNER_STEP * (place + turn * (1 - highest))
        )
        exchange = [
            pltpu.make_async_remote_copy(
                spec_out, spec_in.at[slot], spec_s.at[slot], spec_r.at[slot],
                device_id=device, device_id_type=MESH,
            )
            for slot, device in ((1, before), (0, after))
        ]
        for copy in exchange:
            copy.start()

        for rows in chunks:
            back(spec[rows, :], rows)
        inverse(f_out)
        give(lambda peer: f_out.at[peer], f_in.at[my_row], (ret_s.at[1], ret_r.at[1]))
        give(lambda peer: s_out.at[peer], s_in.at[my_row], (ret_s.at[0], ret_r.at[0]))
        f_in[my_row] = f_out[me]
        s_in[my_row] = s_out[me]

        settle(raw_in, LON - 1, own_r.at[0])

        def products(source, carry):
            s = s_out[source].astype(F32)
            return (
                carry[0] + s * raw_in[source].astype(F32),
                carry[1] + s * y1[source],
            )

        empty = jnp.zeros((MODES, PTS), F32)
        bt, tt = lax.fori_loop(0, LON, products, (empty, empty))

        for copy in exchange:
            copy.wait()
        inner = lat * ROWS + my_row
        has_before, has_after = inner > 0, inner < lats * ROWS - 1
        tu = empty
        for k1 in range(K1):
            rows = pl.ds(k1 * MODES, MODES)
            here = spec[rows, :]
            prev = jnp.where(has_before, spec_in[0, rows, :].astype(F32), 0.0)
            post = jnp.where(has_after, spec_in[1, rows, :].astype(F32), 0.0)
            once = here + kappa * (post - 2.0 * here + prev)
            tu = tu + gains[rows, :] * once * once
        norm_sum = jnp.where(place == 0, norm_sum, 0.0)
        sums = [norm_sum] + [jnp.sum(v, axis=0, keepdims=True) for v in (bt, tt, tu)]
        lane = lax.broadcasted_iota(jnp.int32, (1, PTS), 1)
        packed = jnp.zeros((1, PTS), F32)
        for at, v in enumerate(sums):
            packed = jnp.where(lane == at, jnp.sum(v, axis=1, keepdims=True), packed)
        part[...] = packed

        def send_lat(o, carry):
            pltpu.make_async_remote_copy(
                part, ar1.at[lat], ar_s.at[0], ar_r.at[0],
                device_id=(lax.rem(lat + o, lats), me), device_id_type=MESH,
            ).start()
            return carry

        lax.fori_loop(1, lats, send_lat, 0)
        ar1[lat] = packed
        settle(ar1, lats - 1, ar_r.at[0])
        total = ar1[0]
        for at in range(1, lats):
            total = total + ar1[at]
        mid[...] = total
        give(lambda peer: mid, ar2.at[place], (ar_s.at[1], ar_r.at[1]))
        ar2[place] = total

    def expand(values, r):
        return w_col[r] * jnp.dot(values.T.astype(BF16), e[r], preferred_element_type=F32)

    def arrived(buffer, semaphore):
        @pl.when(owner)
        def _():
            settle(buffer, ROWS - 1, semaphore)

        @pl.when(other)
        def _():
            settle(buffer, ROWS, semaphore)

    arrived(f_in, ret_r.at[1])
    second_halo = halo(f_in, halo_in2, 2)
    arrived(s_in, ret_r.at[0])
    for r in range(ROWS):
        tbuf[r] = expand(s_in[r].astype(F32), r)
    for copy in second_halo:
        copy.wait()
    diffused = diffuse([f_in[r].astype(F32) for r in range(ROWS)], halo_in2)
    for r in range(ROWS):
        ubuf[r] = expand(diffused[r], r)

    arrived(ar2, ar_r.at[1])
    total = ar2[0] + ar2[1] + ar2[2] + ar2[3]
    norm = total[:, 0:1]
    m1, m2, m3 = total[:, 1:2] / norm, total[:, 2:3] / norm, total[:, 3:4] / norm
    alpha = 1.0 / (1.0 + m1)
    spread2 = m2 - m1 * m1
    spread3 = m3 - 3.0 * m1 * m2 + 2.0 * m1 * m1 * m1
    beta = alpha * alpha * spread2
    alpha_next = alpha * spread2 / (spread2 * (1.0 - beta) + alpha * spread3)
    along = alpha * m1 + beta
    x_b, x_t = alpha + alpha_next * along, -alpha_next * alpha
    r_b = alpha * m1 - alpha_next * along
    r_t = -(alpha + alpha_next * (along - alpha))
    r_u = alpha_next * alpha
    rows = [x_b, x_t, r_b, r_t, r_u]
    coefs[...] = jnp.concatenate(
        [jnp.broadcast_to(row, (1, PTS)) for row in rows] + [jnp.zeros((3, PTS), F32)], axis=0
    )

    def sent(rows):
        settle(aux_w, rows, aux_s.at[1])
        settle(got_g.reshape(LON, 8, 128), rows, aux_s.at[0])
        settle(to_owner, rows, own_s.at[0])
        settle(to_owner, rows, own_s.at[1])

    @pl.when(owner)
    def _():
        sent(ROWS - 1)
        settle(s_out, LON - 1, ret_s.at[0])
        settle(f_out, LON - 1, ret_s.at[1])
        settle(ar1, lats - 1, ar_s.at[0])
        settle(ar1, LON - 1, ar_s.at[1])

    @pl.when(other)
    def _():
        sent(ROWS)


def combine(b, t, u, coefs, x_hbm, r_hbm, x, r, sem):
    x_b, x_t, r_b, r_t, r_u = [coefs[at : at + 1, 0:1] for at in range(5)]
    writes = []
    for row in range(ROWS):
        x[row] = x_b * b[row] + x_t * t[row]
        r[row] = r_b * b[row] + r_t * t[row] + r_u * u[row]
        for at, (source, target) in enumerate(((x, x_hbm), (r, r_hbm))):
            write = pltpu.make_async_copy(source.at[row], target.at[row], sem.at[at, row])
            write.start()
            writes.append(write)
    for write in writes:
        write.wait()


def local(right_side, eofs, spectral_gain, diffusivity, flags, counts):
    lats = lax.axis_size("lat")
    wave, twist, pick = tables()
    hbm = pl.BlockSpec(memory_space=pltpu.HBM)
    vmem = pl.BlockSpec(memory_space=pltpu.VMEM)
    like = jax.ShapeDtypeStruct(right_side.shape, F32)
    dma, vm = pltpu.SemaphoreType.DMA, pltpu.VMEM

    def whole(*args):
        kernel(lats, *args)

    fields = pl.pallas_call(
        whole,
        out_shape=(like, like, like, jax.ShapeDtypeStruct((8, PTS), F32)),
        in_specs=[hbm] * 9,
        out_specs=(vmem,) * 4,
        scratch_shapes=[
            vm((ROWS, MODES, COLV), BF16),
            vm((2, KEEP), F32),
            vm((1, MODES), F32),
            vm((ROWS, PTS), jnp.int32),
            vm((ROWS, PTS), jnp.int32),
            vm((2, 2 * PTS, 128), BF16),
            vm((2, 2 * K1, PTS), F32),
            vm((K1, KEEP, 128), BF16),
            vm((ROWS, MODES, PTS), F32),
            vm((ROWS, MODES, PTS), BF16),
            vm((2, 2, MODES, PTS), BF16),
            vm((2, 2, MODES, PTS), BF16),
            vm((8, 128), F32),
            vm((ROWS, 2, PTS), F32),
            vm((LON * 8, 128), F32),
            vm((LON, 2, PTS), F32),
            vm((ROWS, MODES, PTS), BF16),
            vm((LON, MODES, PTS), BF16),
            vm((LON, MODES, PTS), BF16),
            vm((2, SPEC, 2 * PTS), BF16),
            vm((2, SPEC, 2 * PTS), F32),
            vm((SPEC, 128), F32),
            vm((LON, MODES, PTS), F32),
            vm((SPEC, 128), F32),
            vm((SPEC, 128), BF16),
            vm((2, SPEC, 128), BF16),
            vm((LON, MODES, PTS), BF16),
            vm((LON, MODES, PTS), BF16),
            vm((ROWS, MODES, PTS), BF16),
            vm((ROWS, MODES, PTS), BF16),
            vm((1, PTS), F32),
            vm((max(lats, LON), 1, PTS), F32),
            vm((1, PTS), F32),
            vm((ROWS, 1, PTS), F32),
            dma((12,)),
            dma((2,)),
            dma((2,)),
            dma((4,)),
            dma((4,)),
            dma((2,)),
            dma((2,)),
            dma((2,)),
            dma((2,)),
            dma((2,)),
            dma((2,)),
            dma((2,)),
            dma((2,)),
        ],
        compiler_params=pltpu.CompilerParams(
            collective_id=0, has_side_effects=True, vmem_limit_bytes=40 * 2**20
        ),
    )(*[
        pltpu.with_memory_space_constraint(each, pltpu.HBM)
        for each in (
            right_side, jnp.swapaxes(eofs, 1, 2), spectral_gain, diffusivity.reshape(1, MODES),
            flags, counts, wave, twist, pick,
        )
    ])
    return pl.pallas_call(
        combine,
        out_shape=(like, like),
        in_specs=[vmem] * 4,
        out_specs=(hbm, hbm),
        scratch_shapes=[
            vm((ROWS, PTS, COLV), F32),
            vm((ROWS, PTS, COLV), F32),
            dma((2, ROWS)),
        ],
        compiler_params=pltpu.CompilerParams(vmem_limit_bytes=16 * 2**20),
    )(*fields)


def solution(mesh):
    in_specs = (
        P("lat", "lon", None),
        P("lat", None, None),
        P("lon", None),
        P(),
        P("lat", "lon"),
        P("lat", "lon"),
    )
    out_specs = (P("lat", "lon", None), P("lat", "lon", None))
    return jax.shard_map(local, mesh=mesh, in_specs=in_specs, out_specs=out_specs, check_vma=False)
```

```python
import math

import jax
import jax.numpy as jnp
import numpy as np
from jax import lax
from jax.experimental import pallas as pl
from jax.experimental.pallas import tpu as pltpu
from jax.sharding import PartitionSpec as P

MESH = pl.DeviceIdType.MESH
F32, BF16 = jnp.float32, jnp.bfloat16
ROWS, MODES, COLV, NLON, KEEP = 4, 64, 512, 4096, 512
LON, ZS, PTS = 32, 16, 128
K1 = 9
SPEC = K1 * MODES
GROUP = 16
OWNER_FIRST, OWNER_STEP = 2, 8
NEAR = 16

C1, C3, RT = math.cos(math.pi / 8), math.sin(math.pi / 8), math.sqrt(0.5)


def tables():
    kk = np.arange(32)
    signed = np.concatenate([kk, -1 - kk])
    j = np.arange(256)
    angle = 2.0 * np.pi * ((j[:, None] * signed[None, :]) % 256) / 256.0
    cos, sin = np.cos(angle), np.sin(angle)
    re_in = np.concatenate([cos[:, :32], sin[:, :32], cos[:, 32:], sin[:, 32:]], axis=1)
    im_in = np.concatenate([-sin[:, :32], cos[:, :32], -sin[:, 32:], cos[:, 32:]], axis=1)
    wave = np.stack([re_in.reshape(2, PTS, 128), im_in.reshape(2, PTS, 128)], axis=1)
    wave = wave.reshape(2, 2 * PTS, 128)
    k1 = np.arange(K1)
    phase = 2.0 * np.pi * ((k1[:, None] * j[None, :]) % NLON) / NLON
    twist = np.stack([np.cos(phase), np.sin(phase)], axis=1)
    twist = twist.reshape(2 * K1, 2, PTS).transpose(1, 0, 2)
    pick = np.zeros((KEEP, K1, 128))
    for one in range(K1):
        for lane in range(128):
            part, at = lane // 32, lane % 32
            if part < 2:
                k = one + 16 * at
            elif 1 <= one <= 7:
                k = 16 * at + 16 - one
            else:
                continue
            pick[k, one, lane] = (1.0 if k == 0 else 2.0) / NLON
    pick = pick.transpose(1, 0, 2)
    return (
        jnp.asarray(wave.astype(jnp.bfloat16)),
        jnp.asarray(twist.astype(np.float32)),
        jnp.asarray(pick.astype(jnp.bfloat16)),
    )


def cosines(p):
    e = [p[0] + p[8], p[1] + p[7], p[2] + p[6], p[3] + p[5], p[4]]
    o = [p[0] - p[8], p[1] - p[7], p[2] - p[6], p[3] - p[5]]
    f0, f1 = e[0] + e[4], e[1] + e[3]
    f02 = f0 + e[2]
    g0, g1 = e[0] - e[4], RT * (e[1] - e[3])
    o2 = RT * o[2]
    a, b = o[0] + o2, o[0] - o2
    u, v = C1 * o[1] + C3 * o[3], C3 * o[1] - C1 * o[3]
    return [f02 + f1, a + u, g0 + g1, b + v, f0 - e[2], b - v, g0 - g1, a - u, f02 - f1]


def sines(q):
    h = [None, q[1] + q[7], q[2] + q[6], q[3] + q[5], q[4]]
    d = [None, q[1] - q[7], q[2] - q[6], q[3] - q[5]]
    r = RT * (d[1] + d[3])
    h2 = RT * h[2]
    m, n = h2 + h[4], h2 - h[4]
    u, v = C3 * h[1] + C1 * h[3], C1 * h[1] - C3 * h[3]
    return [None, u + m, r + d[2], v + n, d[1] - d[3], v - n, r - d[2], u - m]


def column_of(row, size):
    at = lax.broadcasted_iota(jnp.int32, (size, size), 0)
    to = lax.broadcasted_iota(jnp.int32, (size, size), 1)
    spread = jnp.where(at == to, jnp.broadcast_to(row, (size, size)), 0.0)
    return jnp.sum(spread, axis=1, keepdims=True)


def by_lane(values):
    part = values[:, 0:128] + values[:, 128:256] + values[:, 256:384] + values[:, 384:512]
    return jnp.sum(part, axis=0, keepdims=True)


def kernel(
    lats,
    b_hbm, e_hbm, gain_hbm, kappa_hbm, flags_hbm, counts_hbm, wave_hbm, twist_hbm, pick_hbm,
    b, tbuf, ubuf, coefs,
    e, gain_ref, kappa_ref, flags_ref, counts_ref, wave, twist, pick,
    y0, halo_out, halo_in, halo_in2,
    aux_g, aux_w, got_g, got_w, to_owner, raw_in, rows_in, zbuf, bbuf, gains, y1,
    spec, spec_out, spec_in, s_out, f_out, s_in, f_in, part, ar1, mid, ar2,
    ld, aux_s, aux_r, halo_s, halo_r, own_s, own_r, spec_s, spec_r, ret_s, ret_r, ar_s, ar_r,
):
    lat, me = lax.axis_index("lat"), lax.axis_index("lon")
    spots = [OWNER_FIRST + OWNER_STEP * spot for spot in range(ROWS)]
    owner = (me - spots[0]) * (me - spots[1]) * (me - spots[2]) * (me - spots[3]) == 0
    other = jnp.logical_not(owner)
    place, odd = lax.div(me - OWNER_FIRST, OWNER_STEP), lax.rem(lat, 2)

    def row_at(spot):
        return spot + odd * (ROWS - 1 - 2 * spot)

    my_row = row_at(place)
    down, up = lax.rem(lat + lats - 1, lats), lax.rem(lat + 1, lats)

    small = [
        pltpu.make_async_copy(source, target, ld.at[at])
        for at, (source, target) in enumerate(
            [
                (flags_hbm, flags_ref),
                (counts_hbm, counts_ref),
                (kappa_hbm, kappa_ref),
                (gain_hbm, gain_ref),
            ]
        )
    ]
    loads = [pltpu.make_async_copy(e_hbm, e, ld.at[4])]
    loads += [pltpu.make_async_copy(b_hbm.at[r], b.at[r], ld.at[5 + r]) for r in range(ROWS)]
    owner_loads = [
        pltpu.make_async_copy(wave_hbm, wave, ld.at[9]),
        pltpu.make_async_copy(twist_hbm, twist, ld.at[10]),
        pltpu.make_async_copy(pick_hbm, pick, ld.at[11]),
    ]

    barrier = pltpu.get_barrier_semaphore()

    def greet(device):
        pl.semaphore_signal(barrier, inc=1, device_id=device, device_id_type=MESH)

    @pl.when(owner)
    def _():
        def greet_lon(o, carry):
            greet((lat, lax.rem(me + o, LON)))
            return carry

        def greet_lat(o, carry):
            greet((lax.rem(lat + o, lats), me))
            return carry

        lax.fori_loop(LON // 2, LON, greet_lon, 0)
        lax.fori_loop(1, LON // 2, greet_lon, 0)
        lax.fori_loop(1, lats, greet_lat, 0)

    for load in small + loads:
        load.start()

    @pl.when(owner)
    def _():
        for load in owner_loads:
            load.start()

    @pl.when(other)
    def _():
        for spot in range(ROWS):
            greet((lat, spots[spot]))
        greet((down, me))
        greet((up, me))

    for load in small:
        load.wait()
    flags = flags_ref[...]
    factor = (
        (flags == 0).astype(F32) + 0.5 * (flags == 1).astype(F32) + 0.25 * (flags == 2).astype(F32)
    )
    weight = factor * counts_ref[...].astype(F32) * 0.25
    w_col = [column_of(weight[r : r + 1, :], PTS) for r in range(ROWS)]
    kappa = column_of(kappa_ref[...], MODES)
    for mode in range(2):
        for quarter in range(4):
            at = mode * 4 + quarter
            aux_g[at : at + 1, :] = gain_ref[mode : mode + 1, quarter * 128 : quarter * 128 + 128]

    loads[0].wait()
    norm_part = jnp.zeros((1, PTS), F32)
    for r in range(ROWS):
        loads[1 + r].wait()
        weighted = (w_col[r] * b[r]).astype(BF16)
        modes = lax.dot_general(
            e[r], weighted, (((1,), (1,)), ((), ())), preferred_element_type=F32
        )
        y0[r] = modes
        halo_out[r] = modes.astype(BF16)
        norm_part = norm_part + by_lane(b[r] * b[r])
    for r in range(ROWS):
        aux_w[r] = jnp.concatenate([weight[r : r + 1, :], norm_part], axis=0)

    @pl.when(owner)
    def _():
        pl.semaphore_wait(barrier, LON - 1 + lats - 1)

    @pl.when(other)
    def _():
        pl.semaphore_wait(barrier, ROWS + 2)

    def halo(source, target, at):
        copies = [
            pltpu.make_async_remote_copy(
                source.at[pl.ds(2 * way, 2)], target.at[1 - way],
                halo_s.at[at + way], halo_r.at[at + way],
                device_id=(peer, me), device_id_type=MESH,
            )
            for way, peer in ((0, down), (1, up))
        ]
        for copy in copies:
            copy.start()
        return copies

    def diffuse(rows, halos):
        low, high = lat > 0, lat < lats - 1
        ext = [jnp.where(low, halos[0, i].astype(F32), 0.0) for i in range(2)]
        ext += rows
        ext += [jnp.where(high, halos[1, i].astype(F32), 0.0) for i in range(2)]
        once = [
            ext[i] + kappa * (ext[i + 1] - 2.0 * ext[i] + ext[i - 1]) for i in range(1, 7)
        ]
        once[0] = jnp.where(low, once[0], 0.0)
        once[5] = jnp.where(high, once[5], 0.0)
        return [
            once[i] + kappa * (once[i + 1] - 2.0 * once[i] + once[i - 1]) for i in range(1, 5)
        ]

    first_halo = halo(halo_out, halo_in, 0)

    def to_owners(sends):
        for spot in range(ROWS):
            at, row = spots[spot], row_at(spot)

            @pl.when(me != at)
            def _():
                for source, target, sent, got in sends(row):
                    pltpu.make_async_remote_copy(
                        source, target, sent, got, device_id=(lat, at), device_id_type=MESH
                    ).start()

            @pl.when(me == at)
            def _():
                for source, target, sent, got in sends(row):
                    target[...] = source[...]

    mine8 = pl.ds(pl.multiple_of(8 * me, 8), 8)
    to_owners(
        lambda row: (
            (aux_g, got_g.at[mine8], aux_s.at[0], aux_r.at[0]),
            (aux_w.at[row], got_w.at[me], aux_s.at[1], aux_r.at[1]),
            (halo_out.at[row], raw_in.at[me], own_s.at[0], own_r.at[0]),
        )
    )
    for copy in first_halo:
        copy.wait_recv()
    diffused = diffuse([y0[r] for r in range(ROWS)], halo_in)
    for r in range(ROWS):
        to_owner[r] = diffused[r].astype(BF16)
    to_owners(lambda row: ((to_owner.at[row], rows_in.at[me], own_s.at[1], own_r.at[1]),))

    def settle(buffer, count, semaphore):
        view = buffer.at[pl.ds(0, count)]
        pltpu.make_async_copy(view, view, semaphore).wait()

    def forward(source):
        def one(g, carry):
            c, rows = lax.div(g, 4), pl.ds(pl.multiple_of(lax.rem(g, 4) * GROUP, GROUP), GROUP)
            x = [source[2 * z + c, rows, :].astype(F32) for z in range(ZS)]
            p = [x[0]] + [x[z] + x[16 - z] for z in range(1, 8)] + [x[8]]
            q = [None] + [x[z] - x[16 - z] for z in range(1, 8)]
            real, imag = cosines(p), sines(q)
            for k1 in range(K1):
                to = pl.ds(pl.multiple_of(k1 * MODES + lax.rem(g, 4) * GROUP, GROUP), GROUP)
                if k1 == 0:
                    re, im = real[0], jnp.zeros_like(real[0])
                else:
                    cos = twist[c, pl.ds(2 * k1, 1), :]
                    sin = twist[c, pl.ds(2 * k1 + 1, 1), :]
                    if k1 == 8:
                        re, im = real[8] * cos, real[8] * sin
                    else:
                        re = real[k1] * cos - imag[k1] * sin
                        im = real[k1] * sin + imag[k1] * cos
                zbuf[c, to, 0:PTS] = re.astype(BF16)
                zbuf[c, to, PTS : 2 * PTS] = im.astype(BF16)
            return carry

        lax.fori_loop(0, 8, one, 0, unroll=4)

    def coefficients(rows):
        coef = jnp.dot(zbuf[0, rows, :], wave[0], preferred_element_type=F32)
        return coef + jnp.dot(zbuf[1, rows, :], wave[1], preferred_element_type=F32)

    def back(coef, rows):
        scaled = (coef * gains[rows, :]).astype(BF16)
        for c in range(2):
            bbuf[c, rows, :] = lax.dot_general(
                scaled, wave[c], (((1,), (1,)), ((), ())), preferred_element_type=F32
            )

    chunks = [pl.ds(at * 192, 192) for at in range(3)]

    def inverse(target):
        def one(g, carry):
            c, rows = lax.div(g, 4), pl.ds(pl.multiple_of(lax.rem(g, 4) * GROUP, GROUP), GROUP)
            real, imag = [], [None]
            for k1 in range(K1):
                at = pl.ds(pl.multiple_of(k1 * MODES + lax.rem(g, 4) * GROUP, GROUP), GROUP)
                re = bbuf[c, at, 0:PTS]
                if k1 == 0:
                    real.append(re)
                    continue
                im = bbuf[c, at, PTS : 2 * PTS]
                cos = twist[c, pl.ds(2 * k1, 1), :]
                sin = twist[c, pl.ds(2 * k1 + 1, 1), :]
                real.append(re * cos + im * sin)
                if k1 < 8:
                    imag.append(im * cos - re * sin)
            even, odds = cosines(real), sines(imag)
            target[c, rows, :] = even[0].astype(BF16)
            target[16 + c, rows, :] = even[8].astype(BF16)
            for z in range(1, 8):
                target[2 * z + c, rows, :] = (even[z] + odds[z]).astype(BF16)
                target[2 * (16 - z) + c, rows, :] = (even[z] - odds[z]).astype(BF16)
            return carry

        lax.fori_loop(0, 8, one, 0, unroll=4)

    def give(source_at, target, semaphores, half):
        def send(peer, carry):
            pltpu.make_async_remote_copy(
                source_at(peer), target, semaphores[0], semaphores[1],
                device_id=(lat, peer), device_id_type=MESH,
            ).start()
            return carry

        mine = lax.div(me, NEAR) if half else 1 - lax.div(me, NEAR)
        start, end = half * NEAR, half * NEAR + NEAR
        middle = mine * me + (1 - mine) * end
        lax.fori_loop(start, middle, send, 0)
        lax.fori_loop(middle + mine, end, send, 0)

    def give_f(half):
        give(lambda peer: f_out.at[peer], f_in.at[my_row], (ret_s.at[1], ret_r.at[1]), half)

    def give_s(half):
        give(lambda peer: s_out.at[peer], s_in.at[my_row], (ret_s.at[0], ret_r.at[0]), half)

    @pl.when(owner)
    def _():
        for load in owner_loads:
            load.wait()
        mine = e[my_row]
        gram = lax.dot_general(mine, mine, (((1,), (1,)), ((), ())), preferred_element_type=F32)
        gram_high = gram.astype(BF16)
        gram_low = (gram - gram_high.astype(F32)).astype(BF16)
        gram_both = jnp.concatenate(
            [gram_high.astype(F32), gram_low.astype(F32)], axis=1
        ).astype(BF16)

        settle(got_g.reshape(LON, 8, 128), LON - 1, aux_r.at[0])
        settle(got_w, LON - 1, aux_r.at[1])
        spread = jnp.concatenate([got_g[pl.ds(q, MODES, stride=4), :] for q in range(4)], axis=1)
        first = spread.astype(BF16)
        rest = spread - first.astype(F32)
        second = rest.astype(BF16)
        third = (rest - second.astype(F32)).astype(BF16)
        for k1 in range(K1):
            total = jnp.dot(first, pick[k1], preferred_element_type=F32)
            total = total + jnp.dot(second, pick[k1], preferred_element_type=F32)
            total = total + jnp.dot(third, pick[k1], preferred_element_type=F32)
            gains[pl.ds(k1 * MODES, MODES), :] = total
        norm_sum = got_w[0, 1:2, :]
        for source in range(1, LON):
            norm_sum = norm_sum + got_w[source, 1:2, :]

        settle(rows_in, LON - 1, own_r.at[1])
        forward(rows_in)
        for rows in chunks:
            back(coefficients(rows), rows)
        inverse(s_out)

        for z in range(ZS):
            pair = jnp.concatenate([s_out[2 * z], s_out[2 * z + 1]], axis=1)
            product = jnp.dot(
                gram_both, jnp.concatenate([pair, pair], axis=0), preferred_element_type=F32
            )
            for c in range(2):
                row = got_w[2 * z + c, 0:1, :]
                y1[2 * z + c] = product[:, c * PTS : c * PTS + PTS] * (row * row)
        forward(y1)
        for rows in chunks:
            coef = coefficients(rows)
            spec[rows, :] = coef
            spec_out[rows, :] = coef.astype(BF16)

        lowest, highest = lax.div(ROWS - 1 - my_row, ROWS - 1), lax.div(my_row, ROWS - 1)
        turn = 1 - 2 * odd
        before = (
            lax.rem(lat - lowest + lats, lats), spots[0] + OWNER_STEP * (place - turn * (1 - lowest))
        )
        after = (
            lax.rem(lat + highest, lats), spots[0] + OWNER_STEP * (place + turn * (1 - highest))
        )
        exchange = [
            pltpu.make_async_remote_copy(
                spec_out, spec_in.at[slot], spec_s.at[slot], spec_r.at[slot],
                device_id=device, device_id_type=MESH,
            )
            for slot, device in ((1, before), (0, after))
        ]
        for copy in exchange:
            copy.start()

        for rows in chunks:
            back(spec[rows, :], rows)
        inverse(f_out)
        give_f(0)
        give_f(1)
        f_in[my_row] = f_out[me]
        s_in[my_row] = s_out[me]

        settle(raw_in, LON - 1, own_r.at[0])

        def products(source, carry):
            s = s_out[source].astype(F32)
            return (
                carry[0] + s * raw_in[source].astype(F32),
                carry[1] + s * y1[source],
            )

        empty = jnp.zeros((MODES, PTS), F32)
        bt, tt = lax.fori_loop(0, LON, products, (empty, empty))

        for copy in exchange:
            copy.wait_recv()
        inner = lat * ROWS + my_row
        has_before, has_after = inner > 0, inner < lats * ROWS - 1
        tu = empty
        for k1 in range(K1):
            rows = pl.ds(k1 * MODES, MODES)
            here = spec[rows, :]
            prev = jnp.where(has_before, spec_in[0, rows, :].astype(F32), 0.0)
            post = jnp.where(has_after, spec_in[1, rows, :].astype(F32), 0.0)
            once = here + kappa * (post - 2.0 * here + prev)
            tu = tu + gains[rows, :] * once * once
        norm_sum = jnp.where(place == 0, norm_sum, 0.0)
        sums = [norm_sum] + [jnp.sum(v, axis=0, keepdims=True) for v in (bt, tt, tu)]
        sums = [jnp.sum(v, axis=1, keepdims=True) for v in sums]
        packed = jnp.concatenate([jnp.broadcast_to(v, (1, PTS)) for v in sums], axis=0)
        part[...] = packed

        def send_lat(peer):
            pltpu.make_async_remote_copy(
                part, ar1.at[lat], ar_s.at[0], ar_r.at[0],
                device_id=(peer, me), device_id_type=MESH,
            ).start()

        def by_offset(o, carry):
            send_lat(lax.rem(lat + o, lats))
            return carry

        def by_distance(i, carry):
            j = lax.div(i, 4)
            side = lax.rem(j, 2)
            dy = 4 + (1 - side) * lax.div(j, 2) - side * lax.div(j + 1, 2)
            dx = lax.rem(2 + lax.rem(i, 4), 4)
            x, y = lax.div(lat, 8), lax.rem(lat, 8)
            send_lat(8 * lax.rem(x + dx, 4) + lax.rem(y + dy, 8))
            return carry

        if lats == 32:
            lax.fori_loop(0, 30, by_distance, 0)
            lax.fori_loop(31, 32, by_distance, 0)
        else:
            lax.fori_loop(1, lats, by_offset, 0)
        give_s(0)
        give_s(1)
        ar1[lat] = packed
        settle(ar1, lats - 1, ar_r.at[0])
        total = ar1[0]
        for at in range(1, lats):
            total = total + ar1[at]
        mid[...] = total
        give(lambda peer: mid, ar2.at[place], (ar_s.at[1], ar_r.at[1]), 0)
        give(lambda peer: mid, ar2.at[place], (ar_s.at[1], ar_r.at[1]), 1)
        ar2[place] = total
        for copy in exchange:
            copy.wait_send()

    def expand(values, r):
        return w_col[r] * jnp.dot(values.T.astype(BF16), e[r], preferred_element_type=F32)

    def arrived(buffer, semaphore):
        @pl.when(owner)
        def _():
            settle(buffer, ROWS - 1, semaphore)

        @pl.when(other)
        def _():
            settle(buffer, ROWS, semaphore)

    arrived(f_in, ret_r.at[1])
    second_halo = halo(f_in, halo_in2, 2)
    arrived(s_in, ret_r.at[0])
    for r in range(ROWS):
        tbuf[r] = expand(s_in[r].astype(F32), r)
    for copy in second_halo:
        copy.wait_recv()
    diffused = diffuse([f_in[r].astype(F32) for r in range(ROWS)], halo_in2)
    for r in range(ROWS):
        ubuf[r] = expand(diffused[r], r)

    arrived(ar2, ar_r.at[1])
    total = ar2[0] + ar2[1] + ar2[2] + ar2[3]
    norm = total[0:1]
    m1, m2, m3 = total[1:2] / norm, total[2:3] / norm, total[3:4] / norm
    alpha = 1.0 / (1.0 + m1)
    spread2 = m2 - m1 * m1
    spread3 = m3 - 3.0 * m1 * m2 + 2.0 * m1 * m1 * m1
    beta = alpha * alpha * spread2
    alpha_next = alpha * spread2 / (spread2 * (1.0 - beta) + alpha * spread3)
    along = alpha * m1 + beta
    x_b, x_t = alpha + alpha_next * along, -alpha_next * alpha
    r_b = alpha * m1 - alpha_next * along
    r_t = -(alpha + alpha_next * (along - alpha))
    r_u = alpha_next * alpha
    rows = [x_b, x_t, r_b, r_t, r_u]
    for at, row in enumerate(rows):
        coefs[at : at + 1, :] = jnp.concatenate([row] * (COLV // PTS), axis=1)
    for copy in first_halo + second_halo:
        copy.wait_send()

    def sent(rows):
        settle(aux_w, rows, aux_s.at[1])
        settle(got_g.reshape(LON, 8, 128), rows, aux_s.at[0])
        settle(to_owner, rows, own_s.at[0])
        settle(to_owner, rows, own_s.at[1])

    @pl.when(owner)
    def _():
        sent(ROWS - 1)
        settle(s_out, LON - 1, ret_s.at[0])
        settle(f_out, LON - 1, ret_s.at[1])
        settle(ar1, lats - 1, ar_s.at[0])
        settle(ar1, LON - 1, ar_s.at[1])

    @pl.when(other)
    def _():
        sent(ROWS)


def combine(b, t, u, coefs, x_hbm, r_hbm, x, r, sem):
    x_b, x_t, r_b, r_t, r_u = [coefs[at : at + 1, :] for at in range(5)]
    writes = []
    for row in range(ROWS):
        x[row] = x_b * b[row] + x_t * t[row]
        r[row] = r_b * b[row] + r_t * t[row] + r_u * u[row]
        for at, (source, target) in enumerate(((x, x_hbm), (r, r_hbm))):
            write = pltpu.make_async_copy(source.at[row], target.at[row], sem.at[at, row])
            write.start()
            writes.append(write)
    for write in writes:
        write.wait()


def local(right_side, eofs, spectral_gain, diffusivity, flags, counts):
    lats = lax.axis_size("lat")
    wave, twist, pick = tables()
    hbm = pl.BlockSpec(memory_space=pltpu.HBM)
    vmem = pl.BlockSpec(memory_space=pltpu.VMEM)
    like = jax.ShapeDtypeStruct(right_side.shape, F32)
    dma, vm = pltpu.SemaphoreType.DMA, pltpu.VMEM

    def whole(*args):
        kernel(lats, *args)

    fields = pl.pallas_call(
        whole,
        out_shape=(like, like, like, jax.ShapeDtypeStruct((8, COLV), F32)),
        in_specs=[hbm] * 9,
        out_specs=(vmem,) * 4,
        scratch_shapes=[
            vm((ROWS, MODES, COLV), BF16),
            vm((2, KEEP), F32),
            vm((1, MODES), F32),
            vm((ROWS, PTS), jnp.int32),
            vm((ROWS, PTS), jnp.int32),
            vm((2, 2 * PTS, 128), BF16),
            vm((2, 2 * K1, PTS), F32),
            vm((K1, KEEP, 128), BF16),
            vm((ROWS, MODES, PTS), F32),
            vm((ROWS, MODES, PTS), BF16),
            vm((2, 2, MODES, PTS), BF16),
            vm((2, 2, MODES, PTS), BF16),
            vm((8, 128), F32),
            vm((ROWS, 2, PTS), F32),
            vm((LON * 8, 128), F32),
            vm((LON, 2, PTS), F32),
            vm((ROWS, MODES, PTS), BF16),
            vm((LON, MODES, PTS), BF16),
            vm((LON, MODES, PTS), BF16),
            vm((2, SPEC, 2 * PTS), BF16),
            vm((2, SPEC, 2 * PTS), F32),
            vm((SPEC, 128), F32),
            vm((LON, MODES, PTS), F32),
            vm((SPEC, 128), F32),
            vm((SPEC, 128), BF16),
            vm((2, SPEC, 128), BF16),
            vm((LON, MODES, PTS), BF16),
            vm((LON, MODES, PTS), BF16),
            vm((ROWS, MODES, PTS), BF16),
            vm((ROWS, MODES, PTS), BF16),
            vm((4, PTS), F32),
            vm((max(lats, LON), 4, PTS), F32),
            vm((4, PTS), F32),
            vm((ROWS, 4, PTS), F32),
            dma((12,)),
            dma((2,)),
            dma((2,)),
            dma((4,)),
            dma((4,)),
            dma((2,)),
            dma((2,)),
            dma((2,)),
            dma((2,)),
            dma((2,)),
            dma((2,)),
            dma((2,)),
            dma((2,)),
        ],
        compiler_params=pltpu.CompilerParams(
            collective_id=0, has_side_effects=True, vmem_limit_bytes=40 * 2**20
        ),
    )(*[
        pltpu.with_memory_space_constraint(each, pltpu.HBM)
        for each in (
            right_side, jnp.swapaxes(eofs, 1, 2), spectral_gain, diffusivity.reshape(1, MODES),
            flags, counts, wave, twist, pick,
        )
    ])
    return pl.pallas_call(
        combine,
        out_shape=(like, like),
        in_specs=[vmem] * 4,
        out_specs=(hbm, hbm),
        scratch_shapes=[
            vm((ROWS, PTS, COLV), F32),
            vm((ROWS, PTS, COLV), F32),
            dma((2, ROWS)),
        ],
        compiler_params=pltpu.CompilerParams(vmem_limit_bytes=16 * 2**20),
    )(*fields)


def solution(mesh):
    in_specs = (
        P("lat", "lon", None),
        P("lat", None, None),
        P("lon", None),
        P(),
        P("lat", "lon"),
        P("lat", "lon"),
    )
    out_specs = (P("lat", "lon", None), P("lat", "lon", None))
    return jax.shard_map(local, mesh=mesh, in_specs=in_specs, out_specs=out_specs, check_vma=False)
```

```python
import math

import jax
import jax.numpy as jnp
import numpy as np
from jax import lax
from jax.experimental import pallas as pl
from jax.experimental.pallas import tpu as pltpu
from jax.sharding import PartitionSpec as P

MESH = pl.DeviceIdType.MESH
F32, BF16 = jnp.float32, jnp.bfloat16
ROWS, MODES, COLV, NLON, KEEP = 4, 64, 512, 4096, 512
LON, ZS, PTS = 32, 16, 128
K1 = 9
SPEC = K1 * MODES
GROUP = 16
OWNER_FIRST, OWNER_STEP = 3, 8
NEAR = 16

C1, C3, RT = math.cos(math.pi / 8), math.sin(math.pi / 8), math.sqrt(0.5)


def tables():
    kk = np.arange(32)
    signed = np.concatenate([kk, -1 - kk])
    j = np.arange(256)
    angle = 2.0 * np.pi * ((j[:, None] * signed[None, :]) % 256) / 256.0
    cos, sin = np.cos(angle), np.sin(angle)
    re_in = np.concatenate([cos[:, :32], sin[:, :32], cos[:, 32:], sin[:, 32:]], axis=1)
    im_in = np.concatenate([-sin[:, :32], cos[:, :32], -sin[:, 32:], cos[:, 32:]], axis=1)
    wave = np.stack([re_in.reshape(2, PTS, 128), im_in.reshape(2, PTS, 128)], axis=1)
    wave = wave.reshape(2, 2 * PTS, 128)
    k1 = np.arange(K1)
    phase = 2.0 * np.pi * ((k1[:, None] * j[None, :]) % NLON) / NLON
    twist = np.stack([np.cos(phase), np.sin(phase)], axis=1)
    twist = twist.reshape(2 * K1, 2, PTS).transpose(1, 0, 2)
    pick = np.zeros((KEEP, K1, 128))
    for one in range(K1):
        for lane in range(128):
            part, at = lane // 32, lane % 32
            if part < 2:
                k = one + 16 * at
            elif 1 <= one <= 7:
                k = 16 * at + 16 - one
            else:
                continue
            pick[k, one, lane] = (1.0 if k == 0 else 2.0) / NLON
    pick = pick.transpose(1, 0, 2)
    return (
        jnp.asarray(wave.astype(jnp.bfloat16)),
        jnp.asarray(twist.astype(np.float32)),
        jnp.asarray(pick.astype(jnp.bfloat16)),
    )


def cosines(p):
    e = [p[0] + p[8], p[1] + p[7], p[2] + p[6], p[3] + p[5], p[4]]
    o = [p[0] - p[8], p[1] - p[7], p[2] - p[6], p[3] - p[5]]
    f0, f1 = e[0] + e[4], e[1] + e[3]
    f02 = f0 + e[2]
    g0, g1 = e[0] - e[4], RT * (e[1] - e[3])
    o2 = RT * o[2]
    a, b = o[0] + o2, o[0] - o2
    u, v = C1 * o[1] + C3 * o[3], C3 * o[1] - C1 * o[3]
    return [f02 + f1, a + u, g0 + g1, b + v, f0 - e[2], b - v, g0 - g1, a - u, f02 - f1]


def sines(q):
    h = [None, q[1] + q[7], q[2] + q[6], q[3] + q[5], q[4]]
    d = [None, q[1] - q[7], q[2] - q[6], q[3] - q[5]]
    r = RT * (d[1] + d[3])
    h2 = RT * h[2]
    m, n = h2 + h[4], h2 - h[4]
    u, v = C3 * h[1] + C1 * h[3], C1 * h[1] - C3 * h[3]
    return [None, u + m, r + d[2], v + n, d[1] - d[3], v - n, r - d[2], u - m]


def column_of(row, size):
    at = lax.broadcasted_iota(jnp.int32, (size, size), 0)
    to = lax.broadcasted_iota(jnp.int32, (size, size), 1)
    spread = jnp.where(at == to, jnp.broadcast_to(row, (size, size)), 0.0)
    return jnp.sum(spread, axis=1, keepdims=True)


def by_lane(values):
    part = values[:, 0:128] + values[:, 128:256] + values[:, 256:384] + values[:, 384:512]
    return jnp.sum(part, axis=0, keepdims=True)


def kernel(
    lats,
    b_hbm, e_hbm, gain_hbm, kappa_hbm, flags_hbm, counts_hbm, wave_hbm, twist_hbm, pick_hbm,
    b, tbuf, ubuf, coefs,
    e, gain_ref, kappa_ref, flags_ref, counts_ref, wave, twist, pick,
    y0, halo_out, halo_in, halo_in2,
    aux_g, aux_w, got_g, got_w, to_owner, raw_in, rows_in, zbuf, bbuf, gains, y1,
    spec, spec_out, spec_in, s_out, f_out, s_in, f_in, part, ar1, mid, ar2,
    ld, aux_s, aux_r, halo_s, halo_r, own_s, own_r, spec_s, spec_r, ret_s, ret_r, ar_s, ar_r,
):
    lat, me = lax.axis_index("lat"), lax.axis_index("lon")
    spots = [OWNER_FIRST + OWNER_STEP * spot for spot in range(ROWS)]
    owner = (me - spots[0]) * (me - spots[1]) * (me - spots[2]) * (me - spots[3]) == 0
    other = jnp.logical_not(owner)
    place, odd = lax.div(me - OWNER_FIRST, OWNER_STEP), lax.rem(lat, 2)

    def row_at(spot):
        return spot + odd * (ROWS - 1 - 2 * spot)

    my_row = row_at(place)
    down, up = lax.rem(lat + lats - 1, lats), lax.rem(lat + 1, lats)

    small = [
        pltpu.make_async_copy(source, target, ld.at[at])
        for at, (source, target) in enumerate(
            [
                (flags_hbm, flags_ref),
                (counts_hbm, counts_ref),
                (kappa_hbm, kappa_ref),
                (gain_hbm, gain_ref),
            ]
        )
    ]
    loads = [pltpu.make_async_copy(e_hbm, e, ld.at[4])]
    loads += [pltpu.make_async_copy(b_hbm.at[r], b.at[r], ld.at[5 + r]) for r in range(ROWS)]
    owner_loads = [
        pltpu.make_async_copy(wave_hbm, wave, ld.at[9]),
        pltpu.make_async_copy(twist_hbm, twist, ld.at[10]),
        pltpu.make_async_copy(pick_hbm, pick, ld.at[11]),
    ]

    barrier = pltpu.get_barrier_semaphore()

    def greet(device):
        pl.semaphore_signal(barrier, inc=1, device_id=device, device_id_type=MESH)

    @pl.when(owner)
    def _():
        def greet_lon(o, carry):
            greet((lat, lax.rem(me + o, LON)))
            return carry

        def greet_lat(o, carry):
            greet((lax.rem(lat + o, lats), me))
            return carry

        lax.fori_loop(LON // 2, LON, greet_lon, 0)
        lax.fori_loop(1, LON // 2, greet_lon, 0)
        lax.fori_loop(1, lats, greet_lat, 0)

    for load in small + loads:
        load.start()

    @pl.when(owner)
    def _():
        for load in owner_loads:
            load.start()

    @pl.when(other)
    def _():
        for spot in range(ROWS):
            greet((lat, spots[spot]))
        greet((down, me))
        greet((up, me))

    for load in small:
        load.wait()
    flags = flags_ref[...]
    factor = (
        (flags == 0).astype(F32) + 0.5 * (flags == 1).astype(F32) + 0.25 * (flags == 2).astype(F32)
    )
    weight = factor * counts_ref[...].astype(F32) * 0.25
    w_col = [column_of(weight[r : r + 1, :], PTS) for r in range(ROWS)]
    kappa = column_of(kappa_ref[...], MODES)
    for mode in range(2):
        for quarter in range(4):
            at = mode * 4 + quarter
            aux_g[at : at + 1, :] = gain_ref[mode : mode + 1, quarter * 128 : quarter * 128 + 128]

    loads[0].wait()
    norm_part = jnp.zeros((1, PTS), F32)
    for r in range(ROWS):
        loads[1 + r].wait()
        weighted = (w_col[r] * b[r]).astype(BF16)
        modes = lax.dot_general(
            e[r], weighted, (((1,), (1,)), ((), ())), preferred_element_type=F32
        )
        y0[r] = modes
        halo_out[r] = modes.astype(BF16)
        norm_part = norm_part + by_lane(b[r] * b[r])
    for r in range(ROWS):
        aux_w[r] = jnp.concatenate([weight[r : r + 1, :], norm_part], axis=0)

    @pl.when(owner)
    def _():
        pl.semaphore_wait(barrier, LON - 1 + lats - 1)

    @pl.when(other)
    def _():
        pl.semaphore_wait(barrier, ROWS + 2)

    def halo(source, target, at):
        copies = [
            pltpu.make_async_remote_copy(
                source.at[pl.ds(2 * way, 2)], target.at[1 - way],
                halo_s.at[at + way], halo_r.at[at + way],
                device_id=(peer, me), device_id_type=MESH,
            )
            for way, peer in ((0, down), (1, up))
        ]
        for copy in copies:
            copy.start()
        return copies

    def diffuse(rows, halos):
        low, high = lat > 0, lat < lats - 1
        ext = [jnp.where(low, halos[0, i].astype(F32), 0.0) for i in range(2)]
        ext += rows
        ext += [jnp.where(high, halos[1, i].astype(F32), 0.0) for i in range(2)]
        once = [
            ext[i] + kappa * (ext[i + 1] - 2.0 * ext[i] + ext[i - 1]) for i in range(1, 7)
        ]
        once[0] = jnp.where(low, once[0], 0.0)
        once[5] = jnp.where(high, once[5], 0.0)
        return [
            once[i] + kappa * (once[i + 1] - 2.0 * once[i] + once[i - 1]) for i in range(1, 5)
        ]

    first_halo = halo(halo_out, halo_in, 0)

    def to_owners(sends):
        for spot in range(ROWS):
            at, row = spots[spot], row_at(spot)

            @pl.when(me != at)
            def _():
                for source, target, sent, got in sends(row):
                    pltpu.make_async_remote_copy(
                        source, target, sent, got, device_id=(lat, at), device_id_type=MESH
                    ).start()

            @pl.when(me == at)
            def _():
                for source, target, sent, got in sends(row):
                    target[...] = source[...]

    mine8 = pl.ds(pl.multiple_of(8 * me, 8), 8)
    to_owners(
        lambda row: (
            (aux_g, got_g.at[mine8], aux_s.at[0], aux_r.at[0]),
            (aux_w.at[row], got_w.at[me], aux_s.at[1], aux_r.at[1]),
            (halo_out.at[row], raw_in.at[me], own_s.at[0], own_r.at[0]),
        )
    )
    for copy in first_halo:
        copy.wait_recv()
    diffused = diffuse([y0[r] for r in range(ROWS)], halo_in)
    for r in range(ROWS):
        to_owner[r] = diffused[r].astype(BF16)
    to_owners(lambda row: ((to_owner.at[row], rows_in.at[me], own_s.at[1], own_r.at[1]),))

    def settle(buffer, count, semaphore):
        view = buffer.at[pl.ds(0, count)]
        pltpu.make_async_copy(view, view, semaphore).wait()

    def forward(source):
        def one(g, carry):
            c, rows = lax.div(g, 4), pl.ds(pl.multiple_of(lax.rem(g, 4) * GROUP, GROUP), GROUP)
            x = [source[2 * z + c, rows, :].astype(F32) for z in range(ZS)]
            p = [x[0]] + [x[z] + x[16 - z] for z in range(1, 8)] + [x[8]]
            q = [None] + [x[z] - x[16 - z] for z in range(1, 8)]
            real, imag = cosines(p), sines(q)
            for k1 in range(K1):
                to = pl.ds(pl.multiple_of(k1 * MODES + lax.rem(g, 4) * GROUP, GROUP), GROUP)
                if k1 == 0:
                    re, im = real[0], jnp.zeros_like(real[0])
                else:
                    cos = twist[c, pl.ds(2 * k1, 1), :]
                    sin = twist[c, pl.ds(2 * k1 + 1, 1), :]
                    if k1 == 8:
                        re, im = real[8] * cos, real[8] * sin
                    else:
                        re = real[k1] * cos - imag[k1] * sin
                        im = real[k1] * sin + imag[k1] * cos
                zbuf[c, to, 0:PTS] = re.astype(BF16)
                zbuf[c, to, PTS : 2 * PTS] = im.astype(BF16)
            return carry

        lax.fori_loop(0, 8, one, 0, unroll=4)

    def coefficients(rows):
        coef = jnp.dot(zbuf[0, rows, :], wave[0], preferred_element_type=F32)
        return coef + jnp.dot(zbuf[1, rows, :], wave[1], preferred_element_type=F32)

    def back(coef, rows):
        scaled = (coef * gains[rows, :]).astype(BF16)
        for c in range(2):
            bbuf[c, rows, :] = lax.dot_general(
                scaled, wave[c], (((1,), (1,)), ((), ())), preferred_element_type=F32
            )

    chunks = [pl.ds(at * 192, 192) for at in range(3)]

    def inverse(target):
        def one(g, carry):
            c, rows = lax.div(g, 4), pl.ds(pl.multiple_of(lax.rem(g, 4) * GROUP, GROUP), GROUP)
            real, imag = [], [None]
            for k1 in range(K1):
                at = pl.ds(pl.multiple_of(k1 * MODES + lax.rem(g, 4) * GROUP, GROUP), GROUP)
                re = bbuf[c, at, 0:PTS]
                if k1 == 0:
                    real.append(re)
                    continue
                im = bbuf[c, at, PTS : 2 * PTS]
                cos = twist[c, pl.ds(2 * k1, 1), :]
                sin = twist[c, pl.ds(2 * k1 + 1, 1), :]
                real.append(re * cos + im * sin)
                if k1 < 8:
                    imag.append(im * cos - re * sin)
            even, odds = cosines(real), sines(imag)
            target[c, rows, :] = even[0].astype(BF16)
            target[16 + c, rows, :] = even[8].astype(BF16)
            for z in range(1, 8):
                target[2 * z + c, rows, :] = (even[z] + odds[z]).astype(BF16)
                target[2 * (16 - z) + c, rows, :] = (even[z] - odds[z]).astype(BF16)
            return carry

        lax.fori_loop(0, 8, one, 0, unroll=4)

    def give(source_at, target, semaphores, half):
        def send(peer, carry):
            pltpu.make_async_remote_copy(
                source_at(peer), target, semaphores[0], semaphores[1],
                device_id=(lat, peer), device_id_type=MESH,
            ).start()
            return carry

        mine = lax.div(me, NEAR) if half else 1 - lax.div(me, NEAR)
        start, end = half * NEAR, half * NEAR + NEAR
        middle = mine * me + (1 - mine) * end
        lax.fori_loop(start, middle, send, 0)
        lax.fori_loop(middle + mine, end, send, 0)

    def give_f(half):
        give(lambda peer: f_out.at[peer], f_in.at[my_row], (ret_s.at[1], ret_r.at[1]), half)

    def give_s(half):
        give(lambda peer: s_out.at[peer], s_in.at[my_row], (ret_s.at[0], ret_r.at[0]), half)

    @pl.when(owner)
    def _():
        for load in owner_loads:
            load.wait()
        mine = e[my_row]
        gram = lax.dot_general(mine, mine, (((1,), (1,)), ((), ())), preferred_element_type=F32)
        gram_high = gram.astype(BF16)
        gram_low = (gram - gram_high.astype(F32)).astype(BF16)
        gram_both = jnp.concatenate(
            [gram_high.astype(F32), gram_low.astype(F32)], axis=1
        ).astype(BF16)

        settle(got_g.reshape(LON, 8, 128), LON - 1, aux_r.at[0])
        settle(got_w, LON - 1, aux_r.at[1])
        spread = jnp.concatenate([got_g[pl.ds(q, MODES, stride=4), :] for q in range(4)], axis=1)
        first = spread.astype(BF16)
        rest = spread - first.astype(F32)
        second = rest.astype(BF16)
        third = (rest - second.astype(F32)).astype(BF16)
        for k1 in range(K1):
            total = jnp.dot(first, pick[k1], preferred_element_type=F32)
            total = total + jnp.dot(second, pick[k1], preferred_element_type=F32)
            total = total + jnp.dot(third, pick[k1], preferred_element_type=F32)
            gains[pl.ds(k1 * MODES, MODES), :] = total
        norm_sum = got_w[0, 1:2, :]
        for source in range(1, LON):
            norm_sum = norm_sum + got_w[source, 1:2, :]

        settle(rows_in, LON - 1, own_r.at[1])
        forward(rows_in)
        for rows in chunks:
            back(coefficients(rows), rows)
        inverse(s_out)

        for z in range(ZS):
            pair = jnp.concatenate([s_out[2 * z], s_out[2 * z + 1]], axis=1)
            product = jnp.dot(
                gram_both, jnp.concatenate([pair, pair], axis=0), preferred_element_type=F32
            )
            for c in range(2):
                row = got_w[2 * z + c, 0:1, :]
                y1[2 * z + c] = product[:, c * PTS : c * PTS + PTS] * (row * row)
        forward(y1)
        lowest, highest = lax.div(ROWS - 1 - my_row, ROWS - 1), lax.div(my_row, ROWS - 1)
        turn = 1 - 2 * odd
        before = (
            lax.rem(lat - lowest + lats, lats), spots[0] + OWNER_STEP * (place - turn * (1 - lowest))
        )
        after = (
            lax.rem(lat + highest, lats), spots[0] + OWNER_STEP * (place + turn * (1 - highest))
        )
        for rows in chunks:
            coef = coefficients(rows)
            spec[rows, :] = coef
            spec_out[rows, :] = coef.astype(BF16)
            for slot, device in ((1, before), (0, after)):
                pltpu.make_async_remote_copy(
                    spec_out.at[rows], spec_in.at[slot, rows], spec_s.at[slot], spec_r.at[slot],
                    device_id=device, device_id_type=MESH,
                ).start()

        def exchanged(semaphores):
            for slot in range(2):
                view = spec_in.at[slot]
                pltpu.make_async_copy(view, view, semaphores.at[slot]).wait()

        for rows in chunks:
            back(spec[rows, :], rows)
        inverse(f_out)
        give_f(0)
        give_f(1)
        f_in[my_row] = f_out[me]
        s_in[my_row] = s_out[me]

        settle(raw_in, LON - 1, own_r.at[0])

        def products(source, carry):
            s = s_out[source].astype(F32)
            return (
                carry[0] + s * raw_in[source].astype(F32),
                carry[1] + s * y1[source],
            )

        empty = jnp.zeros((MODES, PTS), F32)
        bt, tt = lax.fori_loop(0, LON, products, (empty, empty))

        exchanged(spec_r)
        inner = lat * ROWS + my_row
        has_before, has_after = inner > 0, inner < lats * ROWS - 1
        tu = empty
        for k1 in range(K1):
            rows = pl.ds(k1 * MODES, MODES)
            here = spec[rows, :]
            prev = jnp.where(has_before, spec_in[0, rows, :].astype(F32), 0.0)
            post = jnp.where(has_after, spec_in[1, rows, :].astype(F32), 0.0)
            once = here + kappa * (post - 2.0 * here + prev)
            tu = tu + gains[rows, :] * once * once
        norm_sum = jnp.where(place == 0, norm_sum, 0.0)
        sums = [norm_sum] + [jnp.sum(v, axis=0, keepdims=True) for v in (bt, tt, tu)]
        sums = [jnp.sum(v, axis=1, keepdims=True) for v in sums]
        packed = jnp.concatenate([jnp.broadcast_to(v, (1, PTS)) for v in sums], axis=0)
        part[...] = packed

        def send_lat(peer):
            pltpu.make_async_remote_copy(
                part, ar1.at[lat], ar_s.at[0], ar_r.at[0],
                device_id=(peer, me), device_id_type=MESH,
            ).start()

        def by_offset(o, carry):
            send_lat(lax.rem(lat + o, lats))
            return carry

        def by_distance(i, carry):
            j = lax.div(i, 4)
            side = lax.rem(j, 2)
            dy = 4 + (1 - side) * lax.div(j, 2) - side * lax.div(j + 1, 2)
            dx = lax.rem(2 + lax.rem(i, 4), 4)
            x, y = lax.div(lat, 8), lax.rem(lat, 8)
            send_lat(8 * lax.rem(x + dx, 4) + lax.rem(y + dy, 8))
            return carry

        if lats == 32:
            lax.fori_loop(0, 30, by_distance, 0)
            lax.fori_loop(31, 32, by_distance, 0)
        else:
            lax.fori_loop(1, lats, by_offset, 0)
        give_s(0)
        give_s(1)
        ar1[lat] = packed
        settle(ar1, lats - 1, ar_r.at[0])
        total = ar1[0]
        for at in range(1, lats):
            total = total + ar1[at]
        mid[...] = total
        give(lambda peer: mid, ar2.at[place], (ar_s.at[1], ar_r.at[1]), 0)
        give(lambda peer: mid, ar2.at[place], (ar_s.at[1], ar_r.at[1]), 1)
        ar2[place] = total
        exchanged(spec_s)

    def expand(values, r):
        return w_col[r] * jnp.dot(values.T.astype(BF16), e[r], preferred_element_type=F32)

    def arrived(buffer, semaphore):
        @pl.when(owner)
        def _():
            settle(buffer, ROWS - 1, semaphore)

        @pl.when(other)
        def _():
            settle(buffer, ROWS, semaphore)

    arrived(f_in, ret_r.at[1])
    second_halo = halo(f_in, halo_in2, 2)
    arrived(s_in, ret_r.at[0])
    for r in range(ROWS):
        tbuf[r] = expand(s_in[r].astype(F32), r)
    for copy in second_halo:
        copy.wait_recv()
    diffused = diffuse([f_in[r].astype(F32) for r in range(ROWS)], halo_in2)
    for r in range(ROWS):
        ubuf[r] = expand(diffused[r], r)

    arrived(ar2, ar_r.at[1])
    total = ar2[0] + ar2[1] + ar2[2] + ar2[3]
    norm = total[0:1]
    m1, m2, m3 = total[1:2] / norm, total[2:3] / norm, total[3:4] / norm
    alpha = 1.0 / (1.0 + m1)
    spread2 = m2 - m1 * m1
    spread3 = m3 - 3.0 * m1 * m2 + 2.0 * m1 * m1 * m1
    beta = alpha * alpha * spread2
    alpha_next = alpha * spread2 / (spread2 * (1.0 - beta) + alpha * spread3)
    along = alpha * m1 + beta
    x_b, x_t = alpha + alpha_next * along, -alpha_next * alpha
    r_b = alpha * m1 - alpha_next * along
    r_t = -(alpha + alpha_next * (along - alpha))
    r_u = alpha_next * alpha
    rows = [x_b, x_t, r_b, r_t, r_u]
    for at, row in enumerate(rows):
        coefs[at : at + 1, :] = jnp.concatenate([row] * (COLV // PTS), axis=1)
    for copy in first_halo + second_halo:
        copy.wait_send()

    def sent(rows):
        settle(aux_w, rows, aux_s.at[1])
        settle(got_g.reshape(LON, 8, 128), rows, aux_s.at[0])
        settle(to_owner, rows, own_s.at[0])
        settle(to_owner, rows, own_s.at[1])

    @pl.when(owner)
    def _():
        sent(ROWS - 1)
        settle(s_out, LON - 1, ret_s.at[0])
        settle(f_out, LON - 1, ret_s.at[1])
        settle(ar1, lats - 1, ar_s.at[0])
        settle(ar1, LON - 1, ar_s.at[1])

    @pl.when(other)
    def _():
        sent(ROWS)


def combine(b, t, u, coefs, x_hbm, r_hbm, x, r, sem):
    x_b, x_t, r_b, r_t, r_u = [coefs[at : at + 1, :] for at in range(5)]
    writes = []
    for row in range(ROWS):
        x[row] = x_b * b[row] + x_t * t[row]
        r[row] = r_b * b[row] + r_t * t[row] + r_u * u[row]
        for at, (source, target) in enumerate(((x, x_hbm), (r, r_hbm))):
            write = pltpu.make_async_copy(source.at[row], target.at[row], sem.at[at, row])
            write.start()
            writes.append(write)
    for write in writes:
        write.wait()


def local(right_side, eofs, spectral_gain, diffusivity, flags, counts):
    lats = lax.axis_size("lat")
    wave, twist, pick = tables()
    hbm = pl.BlockSpec(memory_space=pltpu.HBM)
    vmem = pl.BlockSpec(memory_space=pltpu.VMEM)
    like = jax.ShapeDtypeStruct(right_side.shape, F32)
    dma, vm = pltpu.SemaphoreType.DMA, pltpu.VMEM

    def whole(*args):
        kernel(lats, *args)

    fields = pl.pallas_call(
        whole,
        out_shape=(like, like, like, jax.ShapeDtypeStruct((8, COLV), F32)),
        in_specs=[hbm] * 9,
        out_specs=(vmem,) * 4,
        scratch_shapes=[
            vm((ROWS, MODES, COLV), BF16),
            vm((2, KEEP), F32),
            vm((1, MODES), F32),
            vm((ROWS, PTS), jnp.int32),
            vm((ROWS, PTS), jnp.int32),
            vm((2, 2 * PTS, 128), BF16),
            vm((2, 2 * K1, PTS), F32),
            vm((K1, KEEP, 128), BF16),
            vm((ROWS, MODES, PTS), F32),
            vm((ROWS, MODES, PTS), BF16),
            vm((2, 2, MODES, PTS), BF16),
            vm((2, 2, MODES, PTS), BF16),
            vm((8, 128), F32),
            vm((ROWS, 2, PTS), F32),
            vm((LON * 8, 128), F32),
            vm((LON, 2, PTS), F32),
            vm((ROWS, MODES, PTS), BF16),
            vm((LON, MODES, PTS), BF16),
            vm((LON, MODES, PTS), BF16),
            vm((2, SPEC, 2 * PTS), BF16),
            vm((2, SPEC, 2 * PTS), F32),
            vm((SPEC, 128), F32),
            vm((LON, MODES, PTS), F32),
            vm((SPEC, 128), F32),
            vm((SPEC, 128), BF16),
            vm((2, SPEC, 128), BF16),
            vm((LON, MODES, PTS), BF16),
            vm((LON, MODES, PTS), BF16),
            vm((ROWS, MODES, PTS), BF16),
            vm((ROWS, MODES, PTS), BF16),
            vm((4, PTS), F32),
            vm((max(lats, LON), 4, PTS), F32),
            vm((4, PTS), F32),
            vm((ROWS, 4, PTS), F32),
            dma((12,)),
            dma((2,)),
            dma((2,)),
            dma((4,)),
            dma((4,)),
            dma((2,)),
            dma((2,)),
            dma((2,)),
            dma((2,)),
            dma((2,)),
            dma((2,)),
            dma((2,)),
            dma((2,)),
        ],
        compiler_params=pltpu.CompilerParams(
            collective_id=0, has_side_effects=True, vmem_limit_bytes=40 * 2**20
        ),
    )(*[
        pltpu.with_memory_space_constraint(each, pltpu.HBM)
        for each in (
            right_side, jnp.swapaxes(eofs, 1, 2), spectral_gain, diffusivity.reshape(1, MODES),
            flags, counts, wave, twist, pick,
        )
    ])
    return pl.pallas_call(
        combine,
        out_shape=(like, like),
        in_specs=[vmem] * 4,
        out_specs=(hbm, hbm),
        scratch_shapes=[
            vm((ROWS, PTS, COLV), F32),
            vm((ROWS, PTS, COLV), F32),
            dma((2, ROWS)),
        ],
        compiler_params=pltpu.CompilerParams(vmem_limit_bytes=16 * 2**20),
    )(*fields)


def solution(mesh):
    in_specs = (
        P("lat", "lon", None),
        P("lat", None, None),
        P("lon", None),
        P(),
        P("lat", "lon"),
        P("lat", "lon"),
    )
    out_specs = (P("lat", "lon", None), P("lat", "lon", None))
    return jax.shard_map(local, mesh=mesh, in_specs=in_specs, out_specs=out_specs, check_vma=False)
```
